256 devices in a mesh: lat: 8 (over z), lon: 32 (over x, y, core).
Axes of the slice: x: 4, y: 4, z: 8, core: 2. Of those that a mesh axis runs over, the one named last changes fastest.
Arguments:
- snapshots: bfloat16 [262144, 4096], P(('lat', 'lon')), may hold values from -24 to 24
- test_matrix: bfloat16 [4096, 256], replicated, may hold values from -0.09375 to 0.09375
Outputs:
- basis: float32 [262144, 256], P(('lat', 'lon'))
- projected: float32 [4096, 256], P('lon')
The draws below stay inside these ranges and needn't reach their ends.
All inputs are finite; a program needn't handle non-finite values.
Results may differ from the reference program's by a relative error of at most 0.00037.
Values sent between devices are 32-bit elements; how exact they have to be, the bound alone decides.
A program may use at most 64 MiB of HBM per device.

```python
import jax
import jax.numpy as jnp
from jax import lax

SNAPS = 4096
RANK = 256
GRID = 262144


def with_spikes(array, own_key, source, target, parts, factor):
    owner, partner = [(jnp.arange(array.shape[axis_at]) // (array.shape[axis_at] // parts)).reshape([-1 if axis == axis_at else 1 for axis in range(array.ndim)]) for axis_at in (source, target)]
    chosen = jax.random.permutation(own_key, parts)[partner]
    strong = (owner == chosen) | (owner == (partner + parts // 2) % parts)
    return jnp.where(strong, factor * array, array)


def shard_levels(rng, extent, shards, low, high):
    level = 1.0
    for position, parts in shards:
        steps = jax.random.uniform(jax.random.fold_in(jax.random.fold_in(rng, 6), position), (parts,), jnp.float32, low / len(shards), high / len(shards))
        level = level * jnp.repeat(jnp.exp(steps), extent[position] // parts).reshape((-1,) + (1,) * (len(extent) - 1 - position))
    return level


def bell_draw(key, shape, scale, bound, split=(), dtype=jnp.bfloat16):
    loudness = shard_levels(key, shape, split, -0.22, 0.18) if split else 1.0
    array = jax.random.normal(key, shape, jnp.float32) * scale * loudness
    return jnp.minimum(jnp.maximum(array, -bound), bound).astype(dtype)


def gaussian_with(own_key, extent, scale, reach, cuts, heavy, kind=jnp.bfloat16):
    array = scale * jax.random.normal(own_key, extent, jnp.float32)
    if cuts:
        array = array * shard_levels(own_key, extent, cuts, -0.22, 0.18)
    return jnp.clip(with_spikes(array, jax.random.fold_in(own_key, 3), *heavy), -reach, reach).astype(kind)


def setup_inputs(seed: int = 0) -> dict:
    key_list = jax.random.split(jax.random.key(seed), 3)
    snapshots = gaussian_with(key_list[0], (GRID, SNAPS), 1.0, 24.0, ((0, 256),), (0, 1, 256, 6.0))
    test_matrix = bell_draw(key_list[1], (SNAPS, RANK), SNAPS ** -0.5, 0.09375)
    return {"snapshots": snapshots, "test_matrix": test_matrix}


def reference(snapshots, test_matrix):
    sketch = jnp.dot(snapshots.astype(jnp.float32), test_matrix.astype(jnp.float32), preferred_element_type=jnp.float32)
    gram = jnp.dot(sketch.T, sketch, precision=lax.Precision.HIGHEST)
    lower = jnp.linalg.cholesky(gram)
    basis = jax.scipy.linalg.solve_triangular(lower, sketch.T, lower=True).T
    basis_b = basis.astype(jnp.bfloat16)
    projected = lax.dot_general(snapshots.astype(jnp.float32), basis_b.astype(jnp.float32), (((0,), (0,)), ((), ())), preferred_element_type=jnp.float32)
    return (basis, projected)
```

```python
import functools

import jax
import jax.numpy as jnp
from jax import lax
from jax.experimental import pallas as pl
from jax.experimental.pallas import tpu as pltpu
from jax.sharding import PartitionSpec as P

MESH = pl.DeviceIdType.MESH
HIGHEST = lax.Precision.HIGHEST
f32, bf16 = jnp.float32, jnp.bfloat16
VMEM = pl.BlockSpec(memory_space=pltpu.VMEM)
ANY = pl.BlockSpec(memory_space=pl.ANY)

NX, NY, NZ = 4, 4, 8
ROWS, SNAPS, RANK = 1024, 4096, 256
PARTS = 4
PART = ROWS // PARTS
XY = [(dx, dy) for dx in range(NX) for dy in range(NY)]


def place():
    z, lon = lax.axis_index("lat"), lax.axis_index("lon")
    return lon // 8, (lon // 2) % 4, z, lon % 2


def device(x, y, z, c):
    return (z, (x * NY + y) * 2 + c)


def remote(src, dst, send, recv, where):
    return pltpu.make_async_remote_copy(
        src_ref=src, dst_ref=dst, send_sem=send, recv_sem=recv, device_id=where, device_id_type=MESH
    )


def tn(a, b, precision=None):
    return lax.dot_general(a, b, (((0,), (0,)), ((), ())), precision=precision, preferred_element_type=f32)


def nt(a, b, precision=None):
    return lax.dot_general(a, b, (((1,), (1,)), ((), ())), precision=precision, preferred_element_type=f32)


def greet(partners):
    barrier = pltpu.get_barrier_semaphore()
    for where in partners:
        pl.semaphore_signal(barrier, inc=1, device_id=where, device_id_type=MESH)


def gram_kernel(
    snap_ref, test_ref, sketch_ref, gram_ref,
    snap, test, half, from_core, from_xy, from_z, piece,
    load, cs, cr, xs, xr, zs, zr, gs, gr, hs, hr,
):
    x, y, z, c = place()
    core = device(x, y, z, 1 - c)
    xy = [device((x + dx) % NX, (y + dy) % NY, z, c) for dx, dy in XY[1:]]
    zz = [device(x, y, (z + dz) % NZ, c) for dz in range(1, NZ)]
    greet([core] + xy + zz)

    loads = [pltpu.make_async_copy(test_ref, test, load.at[PARTS])]
    for p in range(PARTS):
        rows = pl.ds(p * PART, PART)
        loads.append(pltpu.make_async_copy(snap_ref.at[rows], snap.at[rows], load.at[p]))
    for copy in loads:
        copy.start()
    loads[0].wait()
    cross = jnp.zeros((RANK, 2 * RANK), f32)
    low = jnp.zeros((RANK, RANK), f32)
    for p in range(PARTS):
        loads[p + 1].wait()
        rows = pl.ds(p * PART, PART)
        s = jnp.dot(snap[rows, :], test[...], preferred_element_type=f32)
        sketch_ref[rows, :] = s
        hi = s.astype(bf16)
        lo = (s - hi.astype(f32)).astype(bf16)
        cross += tn(hi, jnp.concatenate([hi, lo], axis=1))
        low += tn(lo, lo)
    mixed = cross[:, RANK:]
    gram = cross[:, :RANK] + (mixed + mixed.T + low)
    half[0] = gram[:128]
    half[1] = gram[128:]
    pl.semaphore_wait(pltpu.get_barrier_semaphore(), 1 + len(xy) + len(zz))

    copy = remote(half.at[1 - c], from_core, cs, cr, core)
    copy.start()
    copy.wait()
    from_core[...] += half[c]

    mine = x * NY + y
    copies = []
    for k, (dx, dy) in enumerate(XY[1:]):
        to = (x + dx) % NX * NY + (y + dy) % NY
        copy = remote(from_core.at[pl.ds(to * 8, 8)], from_xy.at[k], xs.at[k], xr.at[k], xy[k])
        copy.start()
        copies.append(copy)
    total = from_core[pl.ds(mine * 8, 8), :]
    for k, copy in enumerate(copies):
        copy.wait()
        total += from_xy[k]

    piece[...] = total
    from_z[z] = total
    copies = []
    for k in range(NZ - 1):
        copy = remote(piece, from_z.at[z], zs.at[k], zr.at[k], zz[k])
        copy.start()
        copies.append(copy)
    for copy in copies:
        copy.wait()
    total = from_z[0]
    for k in range(1, NZ):
        total += from_z[k]

    gram_ref[c, pl.ds(mine * 8, 8), :] = total
    copies = []
    for k in range(len(xy)):
        rows = gram_ref.at[c, pl.ds(mine * 8, 8)]
        copy = remote(rows, rows, gs.at[k], gr.at[k], xy[k])
        copy.start()
        copies.append(copy)
    for copy in copies:
        copy.wait()
    copy = remote(gram_ref.at[c], gram_ref.at[c], hs, hr, core)
    copy.start()
    copy.wait()


def factor_block(d, n=64):
    eye = (
        lax.broadcasted_iota(jnp.int32, (n, n), 0) == lax.broadcasted_iota(jnp.int32, (n, n), 1)
    ).astype(f32)
    both = jnp.concatenate([d, eye], axis=1)
    tiles = [both[8 * t : 8 * t + 8] for t in range(n // 8)]
    sub = lax.broadcasted_iota(jnp.int32, (8, 2 * n), 0)
    for k in range(n):
        first, s = divmod(k, 8)
        row = jnp.broadcast_to(tiles[first][s : s + 1, :], (8, 2 * n))
        pivot = jnp.broadcast_to(tiles[first][s : s + 1, k : k + 1], (8, 2 * n))
        scaled = row * (1.0 / pivot)
        for t in range(first, n // 8):
            if t == first and s == 7:
                continue
            column = jnp.broadcast_to(tiles[t][:, k : k + 1], (8, 2 * n))
            if t == first:
                column = jnp.where(sub > s, column, 0.0)
            tiles[t] = tiles[t] - column * scaled
    both = jnp.concatenate(tiles, axis=0)
    diagonal = jnp.sum(both[:, :n] * eye, axis=1, keepdims=True)
    return both[:, n:] * lax.rsqrt(diagonal)


def basis_kernel(gram_ref, sketch_ref, basis_ref, basis_b_ref, work, inverse):
    n = 64
    work[:, :RANK] = gram_ref[...]
    work[:, RANK:] = (
        lax.broadcasted_iota(jnp.int32, (RANK, RANK), 0)
        == lax.broadcasted_iota(jnp.int32, (RANK, RANK), 1)
    ).astype(f32)
    for b in range(RANK // n):
        lo, hi = b * n, (b + 1) * n
        r = jnp.dot(
            factor_block(work[lo:hi, lo:hi]), work[lo:hi, :], precision=HIGHEST, preferred_element_type=f32
        )
        inverse[lo:hi, :] = r[:, RANK:]
        if hi < RANK:
            work[hi:, :] = work[hi:, :] - tn(r[:, hi:RANK], r, HIGHEST)
    basis = nt(sketch_ref[...], inverse[...], HIGHEST)
    basis_ref[...] = basis
    basis_b_ref[...] = basis.astype(bf16)


def project_kernel(
    snap_ref, basis_ref, out_ref,
    snap, flipped, term, from_core, a1, b1, a2, b2, mine, from_z, piece, whole,
    load, cs, cr, a1s, a1r, b1s, b1r, a2s, a2r, b2s, b2r, zs, zr, gs, gr,
):
    x, y, z, c = place()
    core = device(x, y, z, 1 - c)
    xs = [device((x + d) % NX, y, z, c) for d in range(1, NX)]
    ys = [device(x, (y + d) % NY, z, c) for d in range(1, NY)]
    zz = [device(x, y, (z + d) % NZ, c) for d in range(1, NZ)]
    greet([core] + xs + ys + zz)
    for i in range(NX):
        columns = pl.ds((x + 1 + i) % NX * 1024, 1024)
        pltpu.make_async_copy(snap_ref.at[:, columns], snap.at[i], load.at[i]).start()
    flipped[...] = basis_ref[...].T
    pl.semaphore_wait(pltpu.get_barrier_semaphore(), 1 + len(xs) + len(ys) + len(zz))

    for i in range(NX):
        tx = (x + 1 + i) % NX
        pltpu.make_async_copy(snap_ref.at[:, pl.ds(tx * 1024, 1024)], snap.at[i], load.at[i]).wait()
        for j in range(NY):
            ty = (y + 1 + j) % NY
            r = jnp.dot(
                flipped[...], snap[i, :, pl.ds(pl.multiple_of(ty * 256, 256), 256)], preferred_element_type=f32
            )
            term[c, i, j] = r[:, :128]
            term[1 - c, i, j] = r[:, 128:]
            remote(term.at[1, i, j], from_core.at[i, j], cs.at[i, j], cr.at[i, j], core).start()

    first, second = pl.ds(0, 128), pl.ds(128, 128)
    for i in range(NX):
        for j in range(NY):
            copy = remote(term.at[1, i, j], from_core.at[i, j], cs.at[i, j], cr.at[i, j], core)
            copy.wait_recv()
            from_core[i, j] += term[0, i, j]
            if i < 3:
                remote(from_core.at[i, j, first], a1.at[i, j], a1s.at[i, j], a1r.at[i, j], xs[i]).start()
            if j < 3:
                remote(from_core.at[i, j, second], b1.at[j, i], b1s.at[j, i], b1r.at[j, i], ys[j]).start()

    def a_wait(j):
        for i in range(3):
            remote(from_core.at[i, j, first], a1.at[i, j], a1s.at[i, j], a1r.at[i, j], xs[i]).wait_recv()
        return from_core[3, j, :128] + (a1[0, j] + a1[1, j] + a1[2, j])

    def b_wait(i):
        for j in range(3):
            remote(from_core.at[i, j, second], b1.at[j, i], b1s.at[j, i], b1r.at[j, i], ys[j]).wait_recv()
        return from_core[i, 3, 128:] + (b1[0, i] + b1[1, i] + b1[2, i])

    late = []
    for k in range(3):
        a2[0, k] = a_wait(k)
        copy = remote(a2.at[0, k], a2.at[1, k], a2s.at[k], a2r.at[k], ys[k])
        copy.start()
        late.append(copy)
        b2[0, k] = b_wait(k)
        copy = remote(b2.at[0, k], b2.at[1, k], b2s.at[k], b2r.at[k], xs[k])
        copy.start()
        late.append(copy)
    mine[:128] = a_wait(3)
    mine[128:] = b_wait(3)
    for copy in late:
        copy.wait()
    mine[:128] += a2[1, 0] + a2[1, 1] + a2[1, 2]
    mine[128:] += b2[1, 0] + b2[1, 1] + b2[1, 2]

    copies = []
    for k in range(NZ - 1):
        copy = remote(mine.at[pl.ds((z + 1 + k) % NZ * 32, 32)], from_z.at[k], zs.at[k], zr.at[k], zz[k])
        copy.start()
        copies.append(copy)
    total = mine[pl.ds(z * 32, 32), :]
    for k, copy in enumerate(copies):
        copy.wait()
        total += from_z[k]
    piece[...] = total
    whole[pl.ds(z * 32, 32), :] = total
    copies = []
    for k in range(NZ - 1):
        copy = remote(piece, whole.at[pl.ds(z * 32, 32)], gs.at[k], gr.at[k], zz[k])
        copy.start()
        copies.append(copy)
    for copy in copies:
        copy.wait()
    out_ref[...] = whole[...].T

    for i in range(NX):
        for j in range(NY):
            remote(term.at[1, i, j], from_core.at[i, j], cs.at[i, j], cr.at[i, j], core).wait_send()
            if i < 3:
                remote(from_core.at[i, j, first], a1.at[i, j], a1s.at[i, j], a1r.at[i, j], xs[i]).wait_send()
            if j < 3:
                remote(from_core.at[i, j, second], b1.at[j, i], b1s.at[j, i], b1r.at[j, i], ys[j]).wait_send()


def sems(*shape):
    return pltpu.SemaphoreType.DMA(shape) if shape else pltpu.SemaphoreType.DMA


def local(snapshots, test_matrix):
    params = functools.partial(pltpu.CompilerParams, vmem_limit_bytes=56 * 2**20)
    sketch, gram = pl.pallas_call(
        gram_kernel,
        name="gram",
        out_shape=(
            jax.ShapeDtypeStruct((ROWS, RANK), f32),
            jax.ShapeDtypeStruct((2, RANK // 2, RANK), f32),
        ),
        in_specs=[ANY, ANY],
        out_specs=(VMEM, VMEM),
        scratch_shapes=[
            pltpu.VMEM((ROWS, SNAPS), bf16),
            pltpu.VMEM((SNAPS, RANK), bf16),
            pltpu.VMEM((2, 128, RANK), f32),
            pltpu.VMEM((128, RANK), f32),
            pltpu.VMEM((15, 8, RANK), f32),
            pltpu.VMEM((NZ, 8, RANK), f32),
            pltpu.VMEM((8, RANK), f32),
            sems(PARTS + 1),
            sems(), sems(), sems(15), sems(15), sems(7), sems(7), sems(15), sems(15), sems(), sems(),
        ],
        compiler_params=params(collective_id=0, has_side_effects=True),
    )(snapshots, test_matrix)
    basis, basis_b = pl.pallas_call(
        basis_kernel,
        name="basis",
        out_shape=(
            jax.ShapeDtypeStruct((ROWS, RANK), f32),
            jax.ShapeDtypeStruct((ROWS, RANK), bf16),
        ),
        in_specs=[VMEM, VMEM],
        out_specs=(VMEM, VMEM),
        scratch_shapes=[pltpu.VMEM((RANK, 2 * RANK), f32), pltpu.VMEM((RANK, RANK), f32)],
        compiler_params=params(),
    )(gram.reshape(RANK, RANK), sketch)
    projected = pl.pallas_call(
        project_kernel,
        name="project",
        out_shape=jax.ShapeDtypeStruct((128, RANK), f32),
        in_specs=[ANY, VMEM],
        out_specs=VMEM,
        scratch_shapes=[
            pltpu.VMEM((NX, ROWS, 1024), bf16),
            pltpu.VMEM((RANK, ROWS), bf16),
            pltpu.VMEM((2, NX, NY, RANK, 128), f32),
            pltpu.VMEM((NX, NY, RANK, 128), f32),
            pltpu.VMEM((3, NY, 128, 128), f32),
            pltpu.VMEM((3, NX, 128, 128), f32),
            pltpu.VMEM((2, 3, 128, 128), f32),
            pltpu.VMEM((2, 3, 128, 128), f32),
            pltpu.VMEM((RANK, 128), f32),
            pltpu.VMEM((7, 32, 128), f32),
            pltpu.VMEM((32, 128), f32),
            pltpu.VMEM((RANK, 128), f32),
            sems(NX),
            sems(NX, NY), sems(NX, NY),
            sems(3, NY), sems(3, NY), sems(3, NX), sems(3, NX),
            sems(3), sems(3), sems(3), sems(3),
            sems(7), sems(7), sems(7), sems(7),
        ],
        compiler_params=params(collective_id=1, has_side_effects=True),
    )(snapshots, basis_b)
    return basis, projected


def solution(mesh):
    return jax.shard_map(
        local,
        mesh=mesh,
        in_specs=(P(("lat", "lon"), None), P()),
        out_specs=(P(("lat", "lon"), None), P("lon", None)),
        check_vma=False,
    )
```

```python
import functools

import jax
import jax.numpy as jnp
from jax import lax
from jax.experimental import pallas as pl
from jax.experimental.pallas import tpu as pltpu
from jax.sharding import PartitionSpec as P

MESH = pl.DeviceIdType.MESH
HIGHEST = lax.Precision.HIGHEST
f32, bf16 = jnp.float32, jnp.bfloat16
VMEM = pl.BlockSpec(memory_space=pltpu.VMEM)
ANY = pl.BlockSpec(memory_space=pl.ANY)

NX, NY, NZ = 4, 4, 8
ROWS, SNAPS, RANK = 1024, 4096, 256
PARTS = 4
PART = ROWS // PARTS
XY = [(dx, dy) for dx in range(NX) for dy in range(NY)]
ORDER = sorted(XY, key=lambda ij: (max(ij), ij))
RA, RB, RC = 96, 96, 64
RAB = RA + RB


def place():
    z, lon = lax.axis_index("lat"), lax.axis_index("lon")
    return lon // 8, (lon // 2) % 4, z, lon % 2


def device(x, y, z, c):
    return (z, (x * NY + y) * 2 + c)


def remote(src, dst, send, recv, where):
    return pltpu.make_async_remote_copy(
        src_ref=src, dst_ref=dst, send_sem=send, recv_sem=recv, device_id=where, device_id_type=MESH
    )


def tn(a, b, precision=None):
    return lax.dot_general(a, b, (((0,), (0,)), ((), ())), precision=precision, preferred_element_type=f32)


def nt(a, b, precision=None):
    return lax.dot_general(a, b, (((1,), (1,)), ((), ())), precision=precision, preferred_element_type=f32)


def greet(partners):
    barrier = pltpu.get_barrier_semaphore()
    for where in partners:
        pl.semaphore_signal(barrier, inc=1, device_id=where, device_id_type=MESH)


def lanes(v, j):
    return jnp.broadcast_to(v[:, j : j + 1], (8, 128))


def row(v, s):
    return jnp.broadcast_to(v[s : s + 1, :], (8, 128))


def factor_block(d, n=64):
    eye = (
        lax.broadcasted_iota(jnp.int32, (n, n), 0) == lax.broadcasted_iota(jnp.int32, (n, n), 1)
    ).astype(f32)
    both = jnp.concatenate([d, eye], axis=1)
    count = n // 8
    tiles = [both[8 * t : 8 * t + 8] for t in range(count)]
    sub = lax.broadcasted_iota(jnp.int32, (8, 128), 0)
    ahead = [lanes(tiles[0], j) for j in range(8)]
    for p in range(count):
        base = 8 * p
        cols = {p: ahead}
        if p + 1 < count:
            ahead = [lanes(tiles[p + 1], base + 8 + j) for j in range(8)]
        for t in range(p + 1, count):
            cols[t] = [lanes(tiles[t], base + j) for j in range(8)]
        for k in range(8):
            inv = 1.0 / row(cols[p][k], k)
            m = {t: cols[t][k] * inv for t in range(p, count)}
            for j in range(k + 1, 8):
                b = row(cols[p][k], j)
                cols[p][j] = cols[p][j] - (cols[p][k] * b) * inv
                for t in range(p + 1, count):
                    cols[t][j] = cols[t][j] - m[t] * b
            if p + 1 < count:
                for j in range(8):
                    ahead[j] = ahead[j] - m[p + 1] * row(cols[p + 1][k], j)
            pivot_row = row(tiles[p], k)
            if k < 7:
                tiles[p] = tiles[p] - jnp.where(sub > k, m[p], 0.0) * pivot_row
            for t in range(p + 1, count):
                tiles[t] = tiles[t] - m[t] * pivot_row
    both = jnp.concatenate(tiles, axis=0)
    diagonal = jnp.sum(both[:, :n] * eye, axis=1, keepdims=True)
    return both[:, n:] * lax.rsqrt(diagonal)


def kernel(
    snap_ref, test_ref, basis_ref, out_ref,
    snap, test, sketch, basis,
    half, from_core, from_xy, from_z, piece, gram, work, inverse,
    flipped, term, sums, a1, b1, c1, a2, b2, c2, csum, mine, z1, part, whole,
    load, store, gcs, gcr, gxs, gxr, gzs, gzr, gbs, gbr, ghs, ghr,
    cs, cr, a1s, a1r, b1s, b1r, c1s, c1r, a2s, a2r, b2s, b2r, c2s, c2r, zs, zr, ws, wr,
):
    x, y, z, c = place()
    core = device(x, y, z, 1 - c)
    xy = [device((x + dx) % NX, (y + dy) % NY, z, c) for dx, dy in XY[1:]]
    xs = [device((x + d) % NX, y, z, c) for d in range(1, NX)]
    ys = [device(x, (y + d) % NY, z, c) for d in range(1, NY)]
    zz = [device(x, y, (z + dz) % NZ, c) for dz in range(1, NZ)]
    greet([core] + xy + zz)

    loads = [pltpu.make_async_copy(test_ref, test, load.at[PARTS])]
    for p in range(PARTS):
        rows = pl.ds(p * PART, PART)
        loads.append(pltpu.make_async_copy(snap_ref.at[rows], snap.at[rows], load.at[p]))
    for copy in loads:
        copy.start()
    loads[0].wait()
    cross = jnp.zeros((RANK, 2 * RANK), f32)
    low = jnp.zeros((RANK, RANK), f32)
    for p in range(PARTS):
        loads[p + 1].wait()
        rows = pl.ds(p * PART, PART)
        s = jnp.dot(snap[rows, :], test[...], preferred_element_type=f32)
        sketch[rows, :] = s
        hi = s.astype(bf16)
        lo = (s - hi.astype(f32)).astype(bf16)
        cross += tn(hi, jnp.concatenate([hi, lo], axis=1))
        low += tn(lo, lo)
    mixed = cross[:, RANK:]
    term_gram = cross[:, :RANK] + (mixed + mixed.T + low)
    half[0] = term_gram[:128]
    half[1] = term_gram[128:]
    pl.semaphore_wait(pltpu.get_barrier_semaphore(), 1 + len(xy) + len(zz))

    copy = remote(half.at[1 - c], from_core, gcs, gcr, core)
    copy.start()
    copy.wait()
    from_core[...] += half[c]
    own = x * NY + y
    copies = []
    for k, (dx, dy) in enumerate(XY[1:]):
        to = (x + dx) % NX * NY + (y + dy) % NY
        copy = remote(from_core.at[pl.ds(to * 8, 8)], from_xy.at[k], gxs.at[k], gxr.at[k], xy[k])
        copy.start()
        copies.append(copy)
    total = from_core[pl.ds(own * 8, 8), :]
    for k, copy in enumerate(copies):
        copy.wait()
        total += from_xy[k]
    piece[...] = total
    from_z[z] = total
    copies = []
    for k in range(NZ - 1):
        copy = remote(piece, from_z.at[z], gzs.at[k], gzr.at[k], zz[k])
        copy.start()
        copies.append(copy)
    for copy in copies:
        copy.wait()
    total = from_z[0]
    for k in range(1, NZ):
        total += from_z[k]
    gram[c, pl.ds(own * 8, 8), :] = total
    copies = []
    for k in range(len(xy)):
        rows = gram.at[c, pl.ds(own * 8, 8)]
        copy = remote(rows, rows, gbs.at[k], gbr.at[k], xy[k])
        copy.start()
        copies.append(copy)
    for copy in copies:
        copy.wait()
    copy = remote(gram.at[c], gram.at[c], ghs, ghr, core)
    copy.start()
    copy.wait()

    n = 64
    work[:128, :RANK] = gram[0]
    work[128:, :RANK] = gram[1]
    work[:, RANK:] = (
        lax.broadcasted_iota(jnp.int32, (RANK, RANK), 0)
        == lax.broadcasted_iota(jnp.int32, (RANK, RANK), 1)
    ).astype(f32)
    for b in range(RANK // n):
        lo, hi = b * n, (b + 1) * n
        inv = factor_block(work[lo:hi, lo:hi])
        r = jnp.dot(inv, work[lo:hi, :], precision=HIGHEST, preferred_element_type=f32)
        inverse[lo:hi, :] = r[:, RANK:]
        if hi < RANK:
            below = nt(work[hi:, lo:hi], inv, HIGHEST)
            work[hi:, :] = work[hi:, :] - jnp.dot(below, r, precision=HIGHEST, preferred_element_type=f32)

    for p in range(PARTS):
        rows = pl.ds(p * PART, PART)
        s = nt(sketch[rows, :], inverse[...], HIGHEST)
        basis[rows, :] = s
        flipped[:, p * PART : (p + 1) * PART] = s.astype(bf16).T
    out_copy = pltpu.make_async_copy(basis, basis_ref, store)
    out_copy.start()

    to_core, to_x, to_y, to_z = [], [], [], []
    lag = 4
    for step in range(len(ORDER) + lag):
        if step < len(ORDER):
            i, j = ORDER[step]
            chip = (x + 1 + i) % NX * NY + (y + 1 + j) % NY
            r = jnp.dot(
                flipped[...], snap[:, pl.ds(pl.multiple_of(chip * 256, 256), 256)], preferred_element_type=f32
            )
            term[c, step] = r[:, :128]
            term[1 - c, step] = r[:, 128:]
            copy = remote(term.at[1, step], sums.at[step], cs.at[step], cr.at[step], core)
            copy.start()
            to_core.append(copy)
        if step >= lag:
            m = step - lag
            i, j = ORDER[m]
            to_core[m].wait_recv()
            sums[m] += term[0, m]
            if i < 3:
                copy = remote(sums.at[m, pl.ds(0, RA)], a1.at[i, j], a1s.at[i, j], a1r.at[i, j], xs[i])
                copy.start()
                to_x.append(copy)
            if j < 3:
                copy = remote(sums.at[m, pl.ds(RA, RB)], b1.at[j, i], b1s.at[j, i], b1r.at[j, i], ys[j])
                copy.start()
                to_y.append(copy)
            if m % 4 == 3:
                g = m // 4
                for k in range(NZ - 1):
                    rows = pl.ds(pl.multiple_of(RAB + (z + 1 + k) % NZ * 8, 8), 8)
                    copy = remote(
                        sums.at[pl.ds(4 * g, 4), rows], c1.at[k, pl.ds(4 * g, 4)], c1s.at[k, g], c1r.at[k, g], zz[k]
                    )
                    copy.start()
                    to_z.append(copy)

    at = {ij: m for m, ij in enumerate(ORDER)}

    def a_sum(j):
        for i in range(3):
            remote(a1.at[i, j], a1.at[i, j], a1s.at[i, j], a1r.at[i, j], xs[i]).wait_recv()
        return sums[at[3, j], :RA] + (a1[0, j] + a1[1, j] + a1[2, j])

    def b_sum(i):
        for j in range(3):
            remote(b1.at[j, i], b1.at[j, i], b1s.at[j, i], b1r.at[j, i], ys[j]).wait_recv()
        return sums[at[i, 3], RA:RAB] + (b1[0, i] + b1[1, i] + b1[2, i])

    late = []
    for k in range(3):
        a2[0, k] = a_sum(k)
        copy = remote(a2.at[0, k], a2.at[1, k], a2s.at[k], a2r.at[k], ys[k])
        copy.start()
        late.append(copy)
        b2[0, k] = b_sum(k)
        copy = remote(b2.at[0, k], b2.at[1, k], b2s.at[k], b2r.at[k], xs[k])
        copy.start()
        late.append(copy)
    mine[:RA] = a_sum(3)
    mine[RA:] = b_sum(3)

    for copy in to_z:
        copy.wait_recv()
    own_rows = pl.ds(pl.multiple_of(RAB + z * 8, 8), 8)
    total = sums[:, own_rows, :]
    for k in range(NZ - 1):
        total += c1[k]
    csum[...] = total
    to_xy = []
    for k, (dx, dy) in enumerate(XY[1:]):
        m = at[(dx - 1) % 4, (dy - 1) % 4]
        copy = remote(csum.at[m], c2.at[k], c2s.at[k], c2r.at[k], xy[k])
        copy.start()
        to_xy.append(copy)

    for copy in late:
        copy.wait()
    mine[:RA] += a2[1, 0] + a2[1, 1] + a2[1, 2]
    mine[RA:] += b2[1, 0] + b2[1, 1] + b2[1, 2]
    share = RAB // NZ
    copies = []
    for k in range(NZ - 1):
        rows = pl.ds(pl.multiple_of((z + 1 + k) % NZ * share, 8), share)
        copy = remote(mine.at[rows], z1.at[k], zs.at[k], zr.at[k], zz[k])
        copy.start()
        copies.append(copy)
    total = csum[at[3, 3]]
    for k, copy in enumerate(to_xy):
        copy.wait()
        total += c2[k]
    part[share:] = total
    total = mine[pl.ds(pl.multiple_of(z * share, 8), share), :]
    for k, copy in enumerate(copies):
        copy.wait()
        total += z1[k]
    part[:share] = total

    whole[z] = part[...]
    copies = []
    for k in range(NZ - 1):
        copy = remote(part, whole.at[z], ws.at[k], wr.at[k], zz[k])
        copy.start()
        copies.append(copy)
    for copy in copies:
        copy.wait()
    for k in range(NZ):
        out_ref[:, share * k : share * (k + 1)] = whole[k, :share].T
        out_ref[:, RAB + 8 * k : RAB + 8 * (k + 1)] = whole[k, share:].T

    for copy in to_core + to_x + to_y + to_z:
        copy.wait_send()
    out_copy.wait()


def sems(*shape):
    return pltpu.SemaphoreType.DMA(shape) if shape else pltpu.SemaphoreType.DMA


def local(snapshots, test_matrix):
    return pl.pallas_call(
        kernel,
        name="range_finder",
        out_shape=(
            jax.ShapeDtypeStruct((ROWS, RANK), f32),
            jax.ShapeDtypeStruct((128, RANK), f32),
        ),
        in_specs=[ANY, ANY],
        out_specs=(ANY, VMEM),
        scratch_shapes=[
            pltpu.VMEM((ROWS, SNAPS), bf16),
            pltpu.VMEM((SNAPS, RANK), bf16),
            pltpu.VMEM((ROWS, RANK), f32),
            pltpu.VMEM((ROWS, RANK), f32),
            pltpu.VMEM((2, 128, RANK), f32),
            pltpu.VMEM((128, RANK), f32),
            pltpu.VMEM((15, 8, RANK), f32),
            pltpu.VMEM((NZ, 8, RANK), f32),
            pltpu.VMEM((8, RANK), f32),
            pltpu.VMEM((2, 128, RANK), f32),
            pltpu.VMEM((RANK, 2 * RANK), f32),
            pltpu.VMEM((RANK, RANK), f32),
            pltpu.VMEM((RANK, ROWS), bf16),
            pltpu.VMEM((2, 16, RANK, 128), f32),
            pltpu.VMEM((16, RANK, 128), f32),
            pltpu.VMEM((3, NY, RA, 128), f32),
            pltpu.VMEM((3, NX, RB, 128), f32),
            pltpu.VMEM((7, 16, 8, 128), f32),
            pltpu.VMEM((2, 3, RA, 128), f32),
            pltpu.VMEM((2, 3, RB, 128), f32),
            pltpu.VMEM((15, 8, 128), f32),
            pltpu.VMEM((16, 8, 128), f32),
            pltpu.VMEM((RAB, 128), f32),
            pltpu.VMEM((7, RAB // NZ, 128), f32),
            pltpu.VMEM((32, 128), f32),
            pltpu.VMEM((NZ, 32, 128), f32),
            sems(PARTS + 1), sems(),
            sems(), sems(), sems(15), sems(15), sems(7), sems(7), sems(15), sems(15), sems(), sems(),
            sems(16), sems(16),
            sems(3, NY), sems(3, NY), sems(3, NX), sems(3, NX), sems(7, 4), sems(7, 4),
            sems(3), sems(3), sems(3), sems(3), sems(15), sems(15),
            sems(7), sems(7), sems(7), sems(7),
        ],
        compiler_params=pltpu.CompilerParams(
            collective_id=0, has_side_effects=True, vmem_limit_bytes=56 * 2**20
        ),
    )(snapshots, test_matrix)


def solution(mesh):
    return jax.shard_map(
        local,
        mesh=mesh,
        in_specs=(P(("lat", "lon"), None), P()),
        out_specs=(P(("lat", "lon"), None), P("lon", None)),
        check_vma=False,
    )
```

```python
import functools

import jax
import jax.numpy as jnp
from jax import lax
from jax.experimental import pallas as pl
from jax.experimental.pallas import tpu as pltpu
from jax.sharding import PartitionSpec as P

MESH = pl.DeviceIdType.MESH
HIGHEST = lax.Precision.HIGHEST
f32, bf16 = jnp.float32, jnp.bfloat16
VMEM = pl.BlockSpec(memory_space=pltpu.VMEM)
ANY = pl.BlockSpec(memory_space=pl.ANY)

NX, NY, NZ = 4, 4, 8
ROWS, SNAPS, RANK = 1024, 4096, 256
PARTS = 4
PART = ROWS // PARTS
RA, RB, RC = 96, 96, 64
RAB = RA + RB


def place():
    z, lon = lax.axis_index("lat"), lax.axis_index("lon")
    return lax.div(lon, 8), lax.rem(lax.div(lon, 2), 4), z, lax.rem(lon, 2)


def device(x, y, z, c):
    return (z, (x * NY + y) * 2 + c)


def remote(src, dst, send, recv, where):
    return pltpu.make_async_remote_copy(
        src_ref=src, dst_ref=dst, send_sem=send, recv_sem=recv, device_id=where, device_id_type=MESH
    )


def tn(a, b, precision=None):
    return lax.dot_general(a, b, (((0,), (0,)), ((), ())), precision=precision, preferred_element_type=f32)


def nt(a, b, precision=None):
    return lax.dot_general(a, b, (((1,), (1,)), ((), ())), precision=precision, preferred_element_type=f32)


def lanes(v, j):
    return jnp.broadcast_to(v[:, j : j + 1], (8, 128))


def row(v, s):
    return jnp.broadcast_to(v[s : s + 1, :], (8, 128))


def factor_block(d, n=64):
    eye = (
        lax.broadcasted_iota(jnp.int32, (n, n), 0) == lax.broadcasted_iota(jnp.int32, (n, n), 1)
    ).astype(f32)
    both = jnp.concatenate([d, eye], axis=1)
    count = n // 8
    tiles = [both[8 * t : 8 * t + 8] for t in range(count)]
    sub = lax.broadcasted_iota(jnp.int32, (8, 128), 0)
    ahead = [lanes(tiles[0], j) for j in range(8)]
    for p in range(count):
        base = 8 * p
        cols = {p: ahead}
        if p + 1 < count:
            ahead = [lanes(tiles[p + 1], base + 8 + j) for j in range(8)]
        for t in range(p + 1, count):
            cols[t] = [lanes(tiles[t], base + j) for j in range(8)]
        for k in range(8):
            inv = 1.0 / row(cols[p][k], k)
            m = {t: cols[t][k] * inv for t in range(p, count)}
            for j in range(k + 1, 8):
                b = row(cols[p][k], j)
                cols[p][j] = cols[p][j] - (cols[p][k] * b) * inv
                for t in range(p + 1, count):
                    cols[t][j] = cols[t][j] - m[t] * b
            if p + 1 < count:
                for j in range(8):
                    ahead[j] = ahead[j] - m[p + 1] * row(cols[p + 1][k], j)
            pivot_row = row(tiles[p], k)
            if k < 7:
                tiles[p] = tiles[p] - jnp.where(sub > k, m[p], 0.0) * pivot_row
            for t in range(p + 1, count):
                tiles[t] = tiles[t] - m[t] * pivot_row
    both = jnp.concatenate(tiles, axis=0)
    diagonal = jnp.sum(both[:, :n] * eye, axis=1, keepdims=True)
    return both[:, n:] * lax.rsqrt(diagonal)


def kernel(
    snap_ref, test_ref, basis_ref, out_ref,
    snap, test, sketch, basis,
    half, from_core, from_xy, from_z, piece, gram, work, inverse,
    flipped, term, sums, a1, b1, c1, a2, b2, c2, csum, mine, z1,
    load, store, gcs, gcr, gxs, gxr, gzs, gzr, gbs, gbr, ghs, ghr,
    cs, cr, a1s, a1r, b1s, b1r, c1s, c1r, a2s, a2r, b2s, b2r, c2s, c2r, zs, zr, ws, wr,
):
    x, y, z, c = place()
    core = device(x, y, z, 1 - c)

    def along_x(d):
        return device(lax.rem(x + d, NX), y, z, c)

    def along_y(d):
        return device(x, lax.rem(y + d, NY), z, c)

    def along_z(d):
        return device(x, y, lax.rem(z + d, NZ), c)

    def on_plane(k):
        return device(lax.rem(x + lax.div(k, NY), NX), lax.rem(y + lax.rem(k, NY), NY), z, c)

    def loop(first, last, body):
        lax.fori_loop(first, last, lambda k, _: (body(k), 0)[1], 0)

    def part(p):
        rows = pl.ds(pl.multiple_of(p * PART, PART), PART)
        return rows, pltpu.make_async_copy(snap_ref.at[rows], snap.at[rows], load.at[p])

    whole_test = pltpu.make_async_copy(test_ref, test, load.at[PARTS])
    whole_test.start()
    loop(0, PARTS, lambda p: part(p)[1].start())
    barrier = pltpu.get_barrier_semaphore()

    def greet(where):
        pl.semaphore_signal(barrier, inc=1, device_id=where, device_id_type=MESH)

    greet(core)
    loop(1, NX * NY, lambda k: greet(on_plane(k)))
    loop(1, NZ, lambda k: greet(along_z(k)))
    whole_test.wait()

    def sketch_part(p):
        rows, copy = part(p)
        copy.wait()
        sketch[rows, :] = jnp.dot(snap[rows, :], test[...], preferred_element_type=f32)

    loop(0, PARTS, sketch_part)
    hi = sketch[...].astype(bf16)
    lo = (sketch[...] - hi.astype(f32)).astype(bf16)
    cross = tn(hi, jnp.concatenate([hi, lo], axis=1))
    low = tn(lo, lo)
    mixed = cross[:, RANK:]
    term_gram = cross[:, :RANK] + (mixed + mixed.T + low)
    half[0] = term_gram[:128]
    half[1] = term_gram[128:]
    pl.semaphore_wait(barrier, 1 + (NX * NY - 1) + (NZ - 1))

    copy = remote(half.at[1 - c], from_core, gcs, gcr, core)
    copy.start()
    copy.wait()
    from_core[...] += half[c]

    def rows_of(cx, cy):
        return pl.ds(pl.multiple_of((cx * NY + cy) * 8, 8), 8)

    def scatter(k):
        rows = rows_of(lax.rem(x + lax.div(k, NY), NX), lax.rem(y + lax.rem(k, NY), NY))
        remote(from_core.at[rows], from_xy.at[k - 1], gxs, gxr, on_plane(k)).start()

    own = rows_of(x, y)
    loop(1, NX * NY, scatter)
    remote(from_xy, from_xy, gxs, gxr, core).wait()
    total = from_core[own, :]
    for k in range(NX * NY - 1):
        total += from_xy[k]
    piece[...] = total
    loop(1, NZ, lambda k: remote(piece, from_z.at[z], gzs, gzr, along_z(k)).start())
    from_z[z] = total
    remote(from_z.at[pl.ds(0, NZ - 1)], from_z.at[pl.ds(0, NZ - 1)], gzs, gzr, core).wait()
    total = from_z[0]
    for k in range(1, NZ):
        total += from_z[k]
    gram[c, own, :] = total
    mine_of_gram = gram.at[c, own]

    def back(k):
        return remote(mine_of_gram, mine_of_gram, gbs, gbr.at[k - 1], on_plane(k))

    loop(1, NX * NY, lambda k: back(k).start())
    loop(1, NX * NY, lambda k: back(k).wait_recv())
    copy = remote(gram.at[c], gram.at[c], ghs, ghr, core)
    copy.start()
    copy.wait()
    remote(from_xy, from_xy, gbs, gxr, core).wait_send()

    n = 64
    work[:128, :RANK] = gram[0]
    work[128:, :RANK] = gram[1]
    work[:, RANK:] = (
        lax.broadcasted_iota(jnp.int32, (RANK, RANK), 0)
        == lax.broadcasted_iota(jnp.int32, (RANK, RANK), 1)
    ).astype(f32)
    for b in range(RANK // n):
        lo, hi = b * n, (b + 1) * n
        inv = factor_block(work[lo:hi, lo:hi])
        r = jnp.dot(inv, work[lo:hi, :], precision=HIGHEST, preferred_element_type=f32)
        inverse[lo:hi, :] = r[:, RANK:]
        if hi < RANK:
            below = nt(work[hi:, lo:hi], inv, HIGHEST)
            work[hi:, :] = work[hi:, :] - jnp.dot(below, r, precision=HIGHEST, preferred_element_type=f32)

    for p in range(PARTS):
        rows = pl.ds(p * PART, PART)
        s = nt(sketch[rows, :], inverse[...], HIGHEST)
        basis[rows, :] = s
        flipped[:, p * PART : (p + 1) * PART] = s.astype(bf16).T
    out_copy = pltpu.make_async_copy(basis, basis_ref, store)
    out_copy.start()

    to_a, to_b = pl.ds(0, RA), pl.ds(RA, RB)
    blocks = NX * NY
    lag = 4

    def to_core(m):
        return remote(term.at[1, m], sums.at[m], cs, cr.at[m], core)

    def step(n):
        @pl.when(n < blocks)
        def _():
            cx, cy = lax.rem(x + 1 + lax.div(n, NY), NX), lax.rem(y + 1 + lax.rem(n, NY), NY)
            columns = pl.ds(pl.multiple_of((cx * NY + cy) * 256, 256), 256)
            r = jnp.dot(flipped[...], snap[:, columns], preferred_element_type=f32)
            term[c, n] = r[:, :128]
            term[1 - c, n] = r[:, 128:]
            to_core(n).start()

        @pl.when(n >= lag)
        def _():
            m = n - lag
            i, j = lax.div(m, NY), lax.rem(m, NY)
            to_core(m).wait_recv()
            sums[m] += term[0, m]

            @pl.when(i < NX - 1)
            def _():
                remote(sums.at[m, to_a], a1.at[j, i], a1s, a1r.at[j], along_x(i + 1)).start()

            @pl.when(j < NY - 1)
            def _():
                remote(sums.at[m, to_b], b1.at[i, j], b1s, b1r.at[i], along_y(j + 1)).start()

            @pl.when(j == NY - 1)
            def _():
                group = pl.ds(pl.multiple_of(i * NY, NY), NY)

                def to_z(k):
                    rows = pl.ds(pl.multiple_of(RAB + lax.rem(z + k, NZ) * 8, 8), 8)
                    remote(sums.at[group, rows], c1.at[k - 1, group], c1s, c1r, along_z(k)).start()

                loop(1, NZ, to_z)

    loop(0, blocks + lag, step)

    def a_sum(j):
        remote(a1.at[j], a1.at[j], a1s, a1r.at[j], core).wait_recv()
        return sums[(NX - 1) * NY + j, :RA] + (a1[j, 0] + a1[j, 1] + a1[j, 2])

    def b_sum(i):
        remote(b1.at[i], b1.at[i], b1s, b1r.at[i], core).wait_recv()
        return sums[i * NY + NY - 1, RA:RAB] + (b1[i, 0] + b1[i, 1] + b1[i, 2])

    for k in range(3):
        b2[0, k] = b_sum(k)
        remote(b2.at[0, k], b2.at[1, k], b2s, b2r, along_x(k + 1)).start()
    for k in range(3):
        a2[0, k] = a_sum(k)
        remote(a2.at[0, k], a2.at[1, k], a2s, a2r, along_y(k + 1)).start()
    mine[RA:] = b_sum(3)
    mine[:RA] = a_sum(3)
    remote(a2.at[0], a2.at[1], a2s, a2r, core).wait_recv()
    remote(b2.at[0], b2.at[1], b2s, b2r, core).wait_recv()
    mine[:RA] += a2[1, 0] + a2[1, 1] + a2[1, 2]
    mine[RA:] += b2[1, 0] + b2[1, 1] + b2[1, 2]
    share = RAB // NZ

    def to_z1(k):
        rows = pl.ds(pl.multiple_of(lax.rem(z + k, NZ) * share, 8), share)
        remote(mine.at[rows], z1.at[k - 1], zs, zr, along_z(k)).start()

    loop(1, NZ, to_z1)

    remote(c1, c1, c1s, c1r, core).wait_recv()
    own_rows = pl.ds(pl.multiple_of(RAB + z * 8, 8), 8)
    total = sums[:, own_rows, :]
    for k in range(NZ - 1):
        total += c1[k]
    csum[...] = total

    def to_plane(k):
        i = lax.rem(lax.div(k, NY) + NX - 1, NX)
        j = lax.rem(lax.rem(k, NY) + NY - 1, NY)
        remote(csum.at[i * NY + j], c2.at[k - 1], c2s, c2r, on_plane(k)).start()

    loop(1, blocks, to_plane)

    def gather(rows, which):
        def one(k):
            return remote(out_ref.at[rows], out_ref.at[rows], ws.at[which], wr.at[which, k - 1], along_z(k))

        return one

    rows = pl.ds(pl.multiple_of(z * share, 8), share)
    total = mine[rows, :]
    remote(z1, z1, zs, zr, core).wait()
    for k in range(NZ - 1):
        total += z1[k]
    out_ref[rows, :] = total
    large = gather(rows, 0)
    loop(1, NZ, lambda k: large(k).start())
    total = csum[blocks - 1]
    remote(c2, c2, c2s, c2r, core).wait()
    for k in range(blocks - 1):
        total += c2[k]
    out_ref[own_rows, :] = total
    small = gather(own_rows, 1)
    loop(1, NZ, lambda k: small(k).start())
    remote(z1, z1, ws.at[0], zr, core).wait_send()
    remote(c2.at[pl.ds(0, NZ - 1)], c2.at[pl.ds(0, NZ - 1)], ws.at[1], zr, core).wait_send()
    remote(term.at[1], sums, cs, zr, core).wait_send()
    remote(a1, a1, a1s, zr, core).wait_send()
    remote(b1, b1, b1s, zr, core).wait_send()
    remote(c1, c1, c1s, zr, core).wait_send()
    remote(a2.at[0], a2.at[1], a2s, zr, core).wait_send()
    remote(b2.at[0], b2.at[1], b2s, zr, core).wait_send()
    out_copy.wait()
    loop(1, NZ, lambda k: large(k).wait_recv())
    loop(1, NZ, lambda k: small(k).wait_recv())


def sems(*shape):
    return pltpu.SemaphoreType.DMA(shape) if shape else pltpu.SemaphoreType.DMA


def finish(basis_in, flat, basis_ref, out_ref):
    basis_ref[...] = basis_in[...]
    out_ref[...] = flat[...].T


def local(snapshots, test_matrix):
    basis, flat = pl.pallas_call(
        kernel,
        name="range_finder",
        out_shape=(
            jax.ShapeDtypeStruct((ROWS, RANK), f32),
            jax.ShapeDtypeStruct((RANK, 128), f32),
        ),
        in_specs=[ANY, ANY],
        out_specs=(ANY, VMEM),
        scratch_shapes=[
            pltpu.VMEM((ROWS, SNAPS), bf16),
            pltpu.VMEM((SNAPS, RANK), bf16),
            pltpu.VMEM((ROWS, RANK), f32),
            pltpu.VMEM((ROWS, RANK), f32),
            pltpu.VMEM((2, 128, RANK), f32),
            pltpu.VMEM((128, RANK), f32),
            pltpu.VMEM((15, 8, RANK), f32),
            pltpu.VMEM((NZ, 8, RANK), f32),
            pltpu.VMEM((8, RANK), f32),
            pltpu.VMEM((2, 128, RANK), f32),
            pltpu.VMEM((RANK, 2 * RANK), f32),
            pltpu.VMEM((RANK, RANK), f32),
            pltpu.VMEM((RANK, ROWS), bf16),
            pltpu.VMEM((2, 16, RANK, 128), f32),
            pltpu.VMEM((16, RANK, 128), f32),
            pltpu.VMEM((NY, 3, RA, 128), f32),
            pltpu.VMEM((NX, 3, RB, 128), f32),
            pltpu.VMEM((7, 16, 8, 128), f32),
            pltpu.VMEM((2, 3, RA, 128), f32),
            pltpu.VMEM((2, 3, RB, 128), f32),
            pltpu.VMEM((15, 8, 128), f32),
            pltpu.VMEM((16, 8, 128), f32),
            pltpu.VMEM((RAB, 128), f32),
            pltpu.VMEM((7, RAB // NZ, 128), f32),
            sems(PARTS + 1), sems(),
            sems(), sems(), sems(), sems(), sems(), sems(), sems(), sems(15), sems(), sems(),
            sems(), sems(16),
            sems(), sems(NY), sems(), sems(NX), sems(), sems(),
            sems(), sems(), sems(), sems(), sems(), sems(),
            sems(), sems(), sems(2), sems(2, 7),
        ],
        compiler_params=pltpu.CompilerParams(
            collective_id=0, has_side_effects=True, vmem_limit_bytes=56 * 2**20
        ),
    )(snapshots, test_matrix)
    return pl.pallas_call(
        finish,
        name="finish",
        out_shape=(
            jax.ShapeDtypeStruct((ROWS, RANK), f32),
            jax.ShapeDtypeStruct((128, RANK), f32),
        ),
        in_specs=[VMEM, VMEM],
        out_specs=(VMEM, VMEM),
    )(basis, flat)


def solution(mesh):
    return jax.shard_map(
        local,
        mesh=mesh,
        in_specs=(P(("lat", "lon"), None), P()),
        out_specs=(P(("lat", "lon"), None), P("lon", None)),
        check_vma=False,
    )
```

```python
import functools

import jax
import jax.numpy as jnp
from jax import lax
from jax.experimental import pallas as pl
from jax.experimental.pallas import tpu as pltpu
from jax.sharding import PartitionSpec as P

MESH = pl.DeviceIdType.MESH
HIGHEST = lax.Precision.HIGHEST
f32, bf16 = jnp.float32, jnp.bfloat16
VMEM = pl.BlockSpec(memory_space=pltpu.VMEM)
ANY = pl.BlockSpec(memory_space=pl.ANY)

NX, NY, NZ = 4, 4, 8
ROWS, SNAPS, RANK = 1024, 4096, 256
PARTS = 4
PART = ROWS // PARTS
RA, RB, RC = 96, 96, 64
RAB = RA + RB


def place():
    z, lon = lax.axis_index("lat"), lax.axis_index("lon")
    return lax.div(lon, 8), lax.rem(lax.div(lon, 2), 4), z, lax.rem(lon, 2)


def device(x, y, z, c):
    return (z, (x * NY + y) * 2 + c)


def remote(src, dst, send, recv, where):
    return pltpu.make_async_remote_copy(
        src_ref=src, dst_ref=dst, send_sem=send, recv_sem=recv, device_id=where, device_id_type=MESH
    )


def tn(a, b, precision=None):
    return lax.dot_general(a, b, (((0,), (0,)), ((), ())), precision=precision, preferred_element_type=f32)


def nt(a, b, precision=None):
    return lax.dot_general(a, b, (((1,), (1,)), ((), ())), precision=precision, preferred_element_type=f32)


def lanes(v, j):
    return jnp.broadcast_to(v[:, j : j + 1], (8, 128))


def row(v, s):
    return jnp.broadcast_to(v[s : s + 1, :], (8, 128))


def factor_block(d, n=64):
    eye = (
        lax.broadcasted_iota(jnp.int32, (n, n), 0) == lax.broadcasted_iota(jnp.int32, (n, n), 1)
    ).astype(f32)
    both = jnp.concatenate([d, eye], axis=1)
    count = n // 8
    tiles = [both[8 * t : 8 * t + 8] for t in range(count)]
    sub = lax.broadcasted_iota(jnp.int32, (8, 128), 0)
    ahead = [lanes(tiles[0], j) for j in range(8)]
    for p in range(count):
        base = 8 * p
        cols = {p: ahead}
        if p + 1 < count:
            ahead = [lanes(tiles[p + 1], base + 8 + j) for j in range(8)]
        for t in range(p + 1, count):
            cols[t] = [lanes(tiles[t], base + j) for j in range(8)]
        for k in range(8):
            inv = 1.0 / row(cols[p][k], k)
            m = {t: cols[t][k] * inv for t in range(p, count)}
            for j in range(k + 1, 8):
                b = row(cols[p][k], j)
                cols[p][j] = cols[p][j] - (cols[p][k] * b) * inv
                for t in range(p + 1, count):
                    cols[t][j] = cols[t][j] - m[t] * b
            if p + 1 < count:
                for j in range(8):
                    ahead[j] = ahead[j] - m[p + 1] * row(cols[p + 1][k], j)
            pivot_row = row(tiles[p], k)
            if k < 7:
                tiles[p] = tiles[p] - jnp.where(sub > k, m[p], 0.0) * pivot_row
            for t in range(p + 1, count):
                tiles[t] = tiles[t] - m[t] * pivot_row
    both = jnp.concatenate(tiles, axis=0)
    diagonal = jnp.sum(both[:, :n] * eye, axis=1, keepdims=True)
    return both[:, n:] * lax.rsqrt(diagonal)


def kernel(
    snap_ref, test_ref, basis_ref, out_ref,
    snap, test, sketch, split, basis,
    half, from_core, from_xy, from_z, piece, gram, work, inverse,
    flipped, term, sums, a1, b1, c1, a2, b2, c2, csum, mine, z1,
    load, store, gcs, gcr, gxs, gxr, gzs, gzr, gbs, gbr, ghs, ghr,
    cs, cr, a1s, a1r, b1s, b1r, c1s, c1r, a2s, a2r, b2s, b2r, c2s, c2r, zs, zr, ws, wr,
):
    x, y, z, c = place()
    core = device(x, y, z, 1 - c)

    def along_x(d):
        return device(lax.rem(x + d, NX), y, z, c)

    def along_y(d):
        return device(x, lax.rem(y + d, NY), z, c)

    def along_z(d):
        return device(x, y, lax.rem(z + d, NZ), c)

    def on_plane(k):
        return device(lax.rem(x + lax.div(k, NY), NX), lax.rem(y + lax.rem(k, NY), NY), z, c)

    def loop(first, last, body):
        lax.fori_loop(first, last, lambda k, _: (body(k), 0)[1], 0)

    def plane(body):
        loop(0, NX * NY - 1, lambda t: body(1 + lax.rem(25 - t, NX * NY - 1)))

    def ring(body):
        loop(0, NZ - 1, lambda t: body(1 + lax.rem(11 - t, NZ - 1)))

    def part(p):
        rows = pl.ds(pl.multiple_of(p * PART, PART), PART)
        return rows, pltpu.make_async_copy(snap_ref.at[rows], snap.at[rows], load.at[p])

    whole_test = pltpu.make_async_copy(test_ref, test, load.at[PARTS])
    whole_test.start()
    loop(0, PARTS, lambda p: part(p)[1].start())
    barrier = pltpu.get_barrier_semaphore()

    def greet(where):
        pl.semaphore_signal(barrier, inc=1, device_id=where, device_id_type=MESH)

    greet(core)
    plane(lambda k: greet(on_plane(k)))
    ring(lambda k: greet(along_z(k)))
    whole_test.wait()

    def sketch_part(p):
        rows, copy = part(p)
        copy.wait()
        sketch[rows, :] = jnp.dot(snap[rows, :], test[...], preferred_element_type=f32)

    loop(0, PARTS, sketch_part)
    hi = sketch[...].astype(bf16)
    split[0] = hi
    split[1] = (sketch[...] - hi.astype(f32)).astype(bf16)

    def gram_half(h):
        columns = pl.ds(pl.multiple_of(h * 128, 128), 128)
        left = jnp.concatenate([split[0, :, columns], split[1, :, columns]], axis=1)
        r = tn(left, jnp.concatenate([split[0], split[1]], axis=1))
        return (r[:128, :RANK] + r[128:, RANK:]) + (r[:128, RANK:] + r[128:, :RANK])

    halves = remote(half.at[0], from_core, gcs, gcr, core)

    def both_halves(k):
        half[k] = gram_half(lax.rem(c + 1 + k, 2))

        @pl.when(k == 0)
        def _():
            pl.semaphore_wait(barrier, 1 + (NX * NY - 1) + (NZ - 1))
            halves.start()

    loop(0, 2, both_halves)

    halves.wait()
    from_core[...] += half[1]

    def rows_of(cx, cy):
        return pl.ds(pl.multiple_of((cx * NY + cy) * 8, 8), 8)

    def scatter(k):
        rows = rows_of(lax.rem(x + lax.div(k, NY), NX), lax.rem(y + lax.rem(k, NY), NY))
        remote(from_core.at[rows], from_xy.at[k - 1], gxs, gxr, on_plane(k)).start()

    own = rows_of(x, y)
    plane(scatter)
    remote(from_xy, from_xy, gxs, gxr, core).wait()
    total = from_core[own, :]
    for k in range(NX * NY - 1):
        total += from_xy[k]
    piece[...] = total
    ring(lambda k: remote(piece, from_z.at[z], gzs, gzr, along_z(k)).start())
    from_z[z] = total
    remote(from_z.at[pl.ds(0, NZ - 1)], from_z.at[pl.ds(0, NZ - 1)], gzs, gzr, core).wait()
    total = from_z[0]
    for k in range(1, NZ):
        total += from_z[k]
    gram[c, own, :] = total
    mine_of_gram = gram.at[c, own]

    def back(k):
        return remote(mine_of_gram, mine_of_gram, gbs, gbr, on_plane(k))

    plane(lambda k: back(k).start())
    remote(from_xy, from_xy, gbs, gbr, core).wait_recv()
    copy = remote(gram.at[c], gram.at[c], ghs, ghr, core)
    copy.start()
    copy.wait()
    remote(from_xy, from_xy, gbs, gxr, core).wait_send()

    n = 64
    work[:128, :RANK] = gram[0]
    work[128:, :RANK] = gram[1]
    work[:, RANK:] = (
        lax.broadcasted_iota(jnp.int32, (RANK, RANK), 0)
        == lax.broadcasted_iota(jnp.int32, (RANK, RANK), 1)
    ).astype(f32)
    d = work[:n, :n]
    for b in range(RANK // n):
        lo, hi = b * n, (b + 1) * n
        inv = factor_block(d)
        if hi < RANK:
            near = nt(work[hi : hi + n, lo:hi], inv, HIGHEST)
            d = work[hi : hi + n, hi : hi + n] - nt(near, near, HIGHEST)
        r = jnp.dot(inv, work[lo:hi, :], precision=HIGHEST, preferred_element_type=f32)
        inverse[lo:hi, :] = r[:, RANK:]
        if hi < RANK:
            below = nt(work[hi:, lo:hi], inv, HIGHEST)
            work[hi:, :] = work[hi:, :] - jnp.dot(below, r, precision=HIGHEST, preferred_element_type=f32)

    for p in range(PARTS):
        rows = pl.ds(p * PART, PART)
        s = nt(sketch[rows, :], inverse[...], HIGHEST)
        basis[rows, :] = s
        flipped[:, p * PART : (p + 1) * PART] = s.astype(bf16).T
    out_copy = pltpu.make_async_copy(basis, basis_ref, store)
    out_copy.start()

    to_a, to_b = pl.ds(0, RA), pl.ds(RA, RB)
    blocks = NX * NY
    lag = 4

    def to_core(m):
        return remote(term.at[1, m], sums.at[m], cs, cr.at[m], core)

    def step(n):
        @pl.when(n < blocks)
        def _():
            cx, cy = lax.rem(x + 1 + lax.div(n, NY), NX), lax.rem(y + 1 + lax.rem(n, NY), NY)
            columns = pl.ds(pl.multiple_of((cx * NY + cy) * 256, 256), 256)
            r = jnp.dot(flipped[...], snap[:, columns], preferred_element_type=f32)
            term[c, n] = r[:, :128]
            term[1 - c, n] = r[:, 128:]
            to_core(n).start()

        @pl.when(n >= lag)
        def _():
            m = n - lag
            i, j = lax.div(m, NY), lax.rem(m, NY)
            to_core(m).wait_recv()
            sums[m] += term[0, m]

            @pl.when(i < NX - 1)
            def _():
                remote(sums.at[m, to_a], a1.at[j, i], a1s, a1r.at[j], along_x(i + 1)).start()

            @pl.when(j < NY - 1)
            def _():
                remote(sums.at[m, to_b], b1.at[i, j], b1s, b1r.at[i], along_y(j + 1)).start()

            @pl.when(j == NY - 1)
            def _():
                group = pl.ds(pl.multiple_of(i * NY, NY), NY)

                def to_z(k):
                    rows = pl.ds(pl.multiple_of(RAB + lax.rem(z + k, NZ) * 8, 8), 8)
                    remote(sums.at[group, rows], c1.at[k - 1, group], c1s, c1r, along_z(k)).start()

                ring(to_z)

    def steps(g):
        for q in range(4):
            step(g * 4 + q)

    loop(0, (blocks + lag) // 4, steps)

    def a_sum(j):
        remote(a1.at[j], a1.at[j], a1s, a1r.at[j], core).wait_recv()
        return sums[(NX - 1) * NY + j, :RA] + (a1[j, 0] + a1[j, 1] + a1[j, 2])

    def b_sum(i):
        remote(b1.at[i], b1.at[i], b1s, b1r.at[i], core).wait_recv()
        return sums[i * NY + NY - 1, RA:RAB] + (b1[i, 0] + b1[i, 1] + b1[i, 2])

    for k in range(3):
        b2[0, k] = b_sum(k)
        remote(b2.at[0, k], b2.at[1, k], b2s, b2r, along_x(k + 1)).start()
    for k in range(3):
        a2[0, k] = a_sum(k)
        remote(a2.at[0, k], a2.at[1, k], a2s, a2r, along_y(k + 1)).start()
    mine[RA:] = b_sum(3)
    mine[:RA] = a_sum(3)
    remote(a2.at[0], a2.at[1], a2s, a2r, core).wait_recv()
    remote(b2.at[0], b2.at[1], b2s, b2r, core).wait_recv()
    mine[:RA] += a2[1, 0] + a2[1, 1] + a2[1, 2]
    mine[RA:] += b2[1, 0] + b2[1, 1] + b2[1, 2]
    share = RAB // NZ

    def to_z1(k):
        rows = pl.ds(pl.multiple_of(lax.rem(z + k, NZ) * share, 8), share)
        remote(mine.at[rows], z1.at[k - 1], zs, zr, along_z(k)).start()

    ring(to_z1)

    remote(c1, c1, c1s, c1r, core).wait_recv()
    own_rows = pl.ds(pl.multiple_of(RAB + z * 8, 8), 8)
    total = sums[:, own_rows, :]
    for k in range(NZ - 1):
        total += c1[k]
    csum[...] = total

    def to_plane(k):
        i = lax.rem(lax.div(k, NY) + NX - 1, NX)
        j = lax.rem(lax.rem(k, NY) + NY - 1, NY)
        remote(csum.at[i * NY + j], c2.at[k - 1], c2s, c2r, on_plane(k)).start()

    plane(to_plane)

    def gather(rows, which):
        def one(k):
            return remote(out_ref.at[rows], out_ref.at[rows], ws.at[which], wr.at[which], along_z(k))

        return one

    rows = pl.ds(pl.multiple_of(z * share, 8), share)
    total = mine[rows, :]
    remote(z1, z1, zs, zr, core).wait()
    for k in range(NZ - 1):
        total += z1[k]
    out_ref[rows, :] = total
    large = gather(rows, 0)
    ring(lambda k: large(k).start())
    total = csum[blocks - 1]
    remote(c2, c2, c2s, c2r, core).wait()
    for k in range(blocks - 1):
        total += c2[k]
    out_ref[own_rows, :] = total
    small = gather(own_rows, 1)
    ring(lambda k: small(k).start())
    remote(z1, z1, ws.at[0], zr, core).wait_send()
    remote(c2.at[pl.ds(0, NZ - 1)], c2.at[pl.ds(0, NZ - 1)], ws.at[1], zr, core).wait_send()
    remote(term.at[1], sums, cs, zr, core).wait_send()
    remote(a1, a1, a1s, zr, core).wait_send()
    remote(b1, b1, b1s, zr, core).wait_send()
    remote(c1, c1, c1s, zr, core).wait_send()
    remote(a2.at[0], a2.at[1], a2s, zr, core).wait_send()
    remote(b2.at[0], b2.at[1], b2s, zr, core).wait_send()
    out_copy.wait()
    remote(z1, z1, zs, wr.at[0], core).wait_recv()
    remote(c2.at[pl.ds(0, NZ - 1)], c2.at[pl.ds(0, NZ - 1)], zs, wr.at[1], core).wait_recv()


def sems(*shape):
    return pltpu.SemaphoreType.DMA(shape) if shape else pltpu.SemaphoreType.DMA


def finish(basis_in, flat, basis_ref, out_ref):
    basis_ref[...] = basis_in[...]
    out_ref[...] = flat[...].T


def local(snapshots, test_matrix):
    basis, flat = pl.pallas_call(
        kernel,
        name="range_finder",
        out_shape=(
            jax.ShapeDtypeStruct((ROWS, RANK), f32),
            jax.ShapeDtypeStruct((RANK, 128), f32),
        ),
        in_specs=[ANY, ANY],
        out_specs=(ANY, VMEM),
        scratch_shapes=[
            pltpu.VMEM((ROWS, SNAPS), bf16),
            pltpu.VMEM((SNAPS, RANK), bf16),
            pltpu.VMEM((ROWS, RANK), f32),
            pltpu.VMEM((2, ROWS, RANK), bf16),
            pltpu.VMEM((ROWS, RANK), f32),
            pltpu.VMEM((2, 128, RANK), f32),
            pltpu.VMEM((128, RANK), f32),
            pltpu.VMEM((15, 8, RANK), f32),
            pltpu.VMEM((NZ, 8, RANK), f32),
            pltpu.VMEM((8, RANK), f32),
            pltpu.VMEM((2, 128, RANK), f32),
            pltpu.VMEM((RANK, 2 * RANK), f32),
            pltpu.VMEM((RANK, RANK), f32),
            pltpu.VMEM((RANK, ROWS), bf16),
            pltpu.VMEM((2, 16, RANK, 128), f32),
            pltpu.VMEM((16, RANK, 128), f32),
            pltpu.VMEM((NY, 3, RA, 128), f32),
            pltpu.VMEM((NX, 3, RB, 128), f32),
            pltpu.VMEM((7, 16, 8, 128), f32),
            pltpu.VMEM((2, 3, RA, 128), f32),
            pltpu.VMEM((2, 3, RB, 128), f32),
            pltpu.VMEM((15, 8, 128), f32),
            pltpu.VMEM((16, 8, 128), f32),
            pltpu.VMEM((RAB, 128), f32),
            pltpu.VMEM((7, RAB // NZ, 128), f32),
            sems(PARTS + 1), sems(),
            sems(), sems(), sems(), sems(), sems(), sems(), sems(), sems(), sems(), sems(),
            sems(), sems(16),
            sems(), sems(NY), sems(), sems(NX), sems(), sems(),
            sems(), sems(), sems(), sems(), sems(), sems(),
            sems(), sems(), sems(2), sems(2),
        ],
        compiler_params=pltpu.CompilerParams(
            collective_id=0, has_side_effects=True, vmem_limit_bytes=56 * 2**20
        ),
    )(snapshots, test_matrix)
    return pl.pallas_call(
        finish,
        name="finish",
        out_shape=(
            jax.ShapeDtypeStruct((ROWS, RANK), f32),
            jax.ShapeDtypeStruct((128, RANK), f32),
        ),
        in_specs=[VMEM, VMEM],
        out_specs=(VMEM, VMEM),
    )(basis, flat)


def solution(mesh):
    return jax.shard_map(
        local,
        mesh=mesh,
        in_specs=(P(("lat", "lon"), None), P()),
        out_specs=(P(("lat", "lon"), None), P("lon", None)),
        check_vma=False,
    )
```

```python
import functools

import jax
import jax.numpy as jnp
from jax import lax
from jax.experimental import pallas as pl
from jax.experimental.pallas import tpu as pltpu
from jax.sharding import PartitionSpec as P

MESH = pl.DeviceIdType.MESH
HIGHEST = lax.Precision.HIGHEST
f32, bf16 = jnp.float32, jnp.bfloat16
VMEM = pl.BlockSpec(memory_space=pltpu.VMEM)
ANY = pl.BlockSpec(memory_space=pl.ANY)

NX, NY, NZ = 4, 4, 8
ROWS, SNAPS, RANK = 1024, 4096, 256
PARTS = 4
PART = ROWS // PARTS
RA, RB, RC = 96, 96, 64
RAB = RA + RB


def place():
    z, lon = lax.axis_index("lat"), lax.axis_index("lon")
    return lax.div(lon, 8), lax.rem(lax.div(lon, 2), 4), z, lax.rem(lon, 2)


def device(x, y, z, c):
    return (z, (x * NY + y) * 2 + c)


def remote(src, dst, send, recv, where):
    return pltpu.make_async_remote_copy(
        src_ref=src, dst_ref=dst, send_sem=send, recv_sem=recv, device_id=where, device_id_type=MESH
    )


def tn(a, b, precision=None):
    return lax.dot_general(a, b, (((0,), (0,)), ((), ())), precision=precision, preferred_element_type=f32)


def nt(a, b, precision=None):
    return lax.dot_general(a, b, (((1,), (1,)), ((), ())), precision=precision, preferred_element_type=f32)


def lanes(v, j):
    return jnp.broadcast_to(v[:, j : j + 1], (8, 128))


def row(v, s):
    return jnp.broadcast_to(v[s : s + 1, :], (8, 128))


def factor_block(d, n=64):
    eye = (
        lax.broadcasted_iota(jnp.int32, (n, n), 0) == lax.broadcasted_iota(jnp.int32, (n, n), 1)
    ).astype(f32)
    both = jnp.concatenate([d, eye], axis=1)
    count = n // 8
    tiles = [both[8 * t : 8 * t + 8] for t in range(count)]
    sub = lax.broadcasted_iota(jnp.int32, (8, 128), 0)
    ahead = [lanes(tiles[0], j) for j in range(8)]
    for p in range(count):
        base = 8 * p
        cols = {p: ahead}
        if p + 1 < count:
            ahead = [lanes(tiles[p + 1], base + 8 + j) for j in range(8)]
        for t in range(p + 1, count):
            cols[t] = [lanes(tiles[t], base + j) for j in range(8)]
        for k in range(8):
            inv = 1.0 / row(cols[p][k], k)
            m = {t: cols[t][k] * inv for t in range(p, count)}
            for j in range(k + 1, 8):
                b = row(cols[p][k], j)
                cols[p][j] = cols[p][j] - (cols[p][k] * b) * inv
                for t in range(p + 1, count):
                    cols[t][j] = cols[t][j] - m[t] * b
            if p + 1 < count:
                for j in range(8):
                    ahead[j] = ahead[j] - m[p + 1] * row(cols[p + 1][k], j)
            pivot_row = row(tiles[p], k)
            if k < 7:
                tiles[p] = tiles[p] - jnp.where(sub > k, m[p], 0.0) * pivot_row
            for t in range(p + 1, count):
                tiles[t] = tiles[t] - m[t] * pivot_row
    both = jnp.concatenate(tiles, axis=0)
    diagonal = jnp.sum(both[:, :n] * eye, axis=1, keepdims=True)
    return both[:, n:] * lax.rsqrt(diagonal)


def kernel(
    snap_ref, test_ref, basis_ref, out_ref,
    snap, test, sketch, split, basis,
    half, from_core, from_xy, from_z, piece, gram, work, inverse,
    flipped, term, sums, a1, b1, c1, a2, b2, c2, csum, mine, z1,
    load, store, gcs, gcr, gxs, gxr, gzs, gzr, gbs, gbr, ghs, ghr,
    cs, cr, a1s, a1r, b1s, b1r, c1s, c1r, a2s, a2r, b2s, b2r, c2s, c2r, zs, zr, ws, wr,
):
    x, y, z, c = place()
    core = device(x, y, z, 1 - c)

    def along_x(d):
        return device(lax.rem(x + d, NX), y, z, c)

    def along_y(d):
        return device(x, lax.rem(y + d, NY), z, c)

    def along_z(d):
        return device(x, y, lax.rem(z + d, NZ), c)

    def on_plane(k):
        return device(lax.rem(x + lax.div(k, NY), NX), lax.rem(y + lax.rem(k, NY), NY), z, c)

    def loop(first, last, body):
        lax.fori_loop(first, last, lambda k, _: (body(k), 0)[1], 0)

    def plane(body):
        loop(0, NX * NY - 1, lambda t: body(1 + lax.rem(25 - t, NX * NY - 1)))

    def ring(body):
        loop(0, NZ - 1, lambda t: body(1 + lax.rem(11 - t, NZ - 1)))

    def part(p):
        rows = pl.ds(pl.multiple_of(p * PART, PART), PART)
        return rows, pltpu.make_async_copy(snap_ref.at[rows], snap.at[rows], load.at[p])

    whole_test = pltpu.make_async_copy(test_ref, test, load.at[PARTS])
    whole_test.start()
    loop(0, PARTS, lambda p: part(p)[1].start())
    barrier = pltpu.get_barrier_semaphore()

    def greet(where):
        pl.semaphore_signal(barrier, inc=1, device_id=where, device_id_type=MESH)

    greet(core)
    plane(lambda k: greet(on_plane(k)))
    ring(lambda k: greet(along_z(k)))
    whole_test.wait()

    def sketch_part(p):
        rows, copy = part(p)
        copy.wait()
        sketch[rows, :] = jnp.dot(snap[rows, :], test[...], preferred_element_type=f32)

    loop(0, PARTS, sketch_part)
    hi = sketch[...].astype(bf16)
    split[0] = hi
    split[1] = (sketch[...] - hi.astype(f32)).astype(bf16)

    def gram_half(h):
        columns = pl.ds(pl.multiple_of(h * 128, 128), 128)
        left = jnp.concatenate([split[0, :, columns], split[1, :, columns]], axis=1)
        r = tn(left, jnp.concatenate([split[0], split[1]], axis=1))
        return (r[:128, :RANK] + r[128:, RANK:]) + (r[:128, RANK:] + r[128:, :RANK])

    halves = remote(half.at[0], from_core, gcs, gcr, core)

    def both_halves(k):
        half[k] = gram_half(lax.rem(c + 1 + k, 2))

        @pl.when(k == 0)
        def _():
            pl.semaphore_wait(barrier, 1 + (NX * NY - 1) + (NZ - 1))
            halves.start()

    loop(0, 2, both_halves)

    work[:, RANK:] = (
        lax.broadcasted_iota(jnp.int32, (RANK, RANK), 0)
        == lax.broadcasted_iota(jnp.int32, (RANK, RANK), 1)
    ).astype(f32)
    halves.wait()
    from_core[...] += half[1]

    def rows_of(cx, cy):
        return pl.ds(pl.multiple_of((cx * NY + cy) * 8, 8), 8)

    def scatter(k):
        rows = rows_of(lax.rem(x + lax.div(k, NY), NX), lax.rem(y + lax.rem(k, NY), NY))
        remote(from_core.at[rows], from_xy.at[k - 1], gxs, gxr, on_plane(k)).start()

    own = rows_of(x, y)
    plane(scatter)
    remote(from_xy, from_xy, gxs, gxr, core).wait()
    total = from_core[own, :]
    for k in range(NX * NY - 1):
        total += from_xy[k]
    piece[...] = total
    ring(lambda k: remote(piece, from_z.at[z], gzs, gzr, along_z(k)).start())
    from_z[z] = total
    remote(from_z.at[pl.ds(0, NZ - 1)], from_z.at[pl.ds(0, NZ - 1)], gzs, gzr, core).wait()
    total = from_z[0]
    for k in range(1, NZ):
        total += from_z[k]
    gram[c, own, :] = total
    mine_of_gram = gram.at[c, own]

    def back(k):
        return remote(mine_of_gram, mine_of_gram, gbs, gbr, on_plane(k))

    plane(lambda k: back(k).start())
    remote(from_xy, from_xy, gbs, gbr, core).wait_recv()
    copy = remote(gram.at[c], gram.at[c], ghs, ghr, core)
    copy.start()
    copy.wait()
    remote(from_xy, from_xy, gbs, gxr, core).wait_send()

    n = 64
    work[:128, :RANK] = gram[0]
    work[128:, :RANK] = gram[1]
    d = work[:n, :n]
    for b in range(RANK // n):
        lo, hi = b * n, (b + 1) * n
        inv = factor_block(d)
        if hi < RANK:
            near = nt(work[hi : hi + n, lo:hi], inv, HIGHEST)
            d = work[hi : hi + n, hi : hi + n] - nt(near, near, HIGHEST)
        r = jnp.dot(inv, work[lo:hi, :], precision=HIGHEST, preferred_element_type=f32)
        inverse[lo:hi, :] = r[:, RANK:]
        if hi < RANK:
            below = nt(work[hi:, lo:hi], inv, HIGHEST)
            work[hi:, :] = work[hi:, :] - jnp.dot(below, r, precision=HIGHEST, preferred_element_type=f32)

    for p in range(PARTS):
        rows = pl.ds(p * PART, PART)
        s = nt(sketch[rows, :], inverse[...], HIGHEST)
        basis[rows, :] = s
        flipped[:, p * PART : (p + 1) * PART] = s.astype(bf16).T
    out_copy = pltpu.make_async_copy(basis, basis_ref, store)
    out_copy.start()

    def off(i):
        h, r = lax.div(i, 2), lax.rem(i, 2)
        return 2 - r + h * (1 + 2 * r)

    to_a, to_b = pl.ds(0, RA), pl.ds(RA, RB)
    blocks = NX * NY
    lag = 4

    def to_core(m):
        return remote(term.at[1, m], sums.at[m], cs, cr.at[m], core)

    def step(n):
        @pl.when(n < blocks)
        def _():
            cx, cy = lax.rem(x + off(lax.div(n, NY)), NX), lax.rem(y + off(lax.rem(n, NY)), NY)
            columns = pl.ds(pl.multiple_of((cx * NY + cy) * 256, 256), 256)
            r = jnp.dot(flipped[...], snap[:, columns], preferred_element_type=f32)
            term[c, n] = r[:, :128]
            term[1 - c, n] = r[:, 128:]
            to_core(n).start()

        @pl.when(n >= lag)
        def _():
            m = n - lag
            i, j = lax.div(m, NY), lax.rem(m, NY)
            to_core(m).wait_recv()
            sums[m] += term[0, m]

            @pl.when(i < NX - 1)
            def _():
                remote(sums.at[m, to_a], a1.at[j, i], a1s, a1r.at[j], along_x(off(i))).start()

            @pl.when(j < NY - 1)
            def _():
                remote(sums.at[m, to_b], b1.at[i, j], b1s, b1r.at[i], along_y(off(j))).start()

            @pl.when(j == NY - 1)
            def _():
                group = pl.ds(pl.multiple_of(i * NY, NY), NY)

                def to_z(k):
                    rows = pl.ds(pl.multiple_of(RAB + lax.rem(z + k, NZ) * 8, 8), 8)
                    remote(sums.at[group, rows], c1.at[k - 1, group], c1s, c1r, along_z(k)).start()

                ring(to_z)

    def steps(g):
        for q in range(4):
            step(g * 4 + q)

    loop(0, (blocks + lag) // 4, steps)

    def a_sum(j):
        remote(a1.at[j], a1.at[j], a1s, a1r.at[j], core).wait_recv()
        return sums[(NX - 1) * NY + j, :RA] + (a1[j, 0] + a1[j, 1] + a1[j, 2])

    def b_sum(i):
        remote(b1.at[i], b1.at[i], b1s, b1r.at[i], core).wait_recv()
        return sums[i * NY + NY - 1, RA:RAB] + (b1[i, 0] + b1[i, 1] + b1[i, 2])

    near = (2, 1, 3)
    for k in range(3):
        b2[0, k] = b_sum(k)
        remote(b2.at[0, k], b2.at[1, k], b2s, b2r, along_x(near[k])).start()
    for k in range(3):
        a2[0, k] = a_sum(k)
        remote(a2.at[0, k], a2.at[1, k], a2s, a2r, along_y(near[k])).start()
    mine[RA:] = b_sum(3)
    mine[:RA] = a_sum(3)
    remote(a2.at[0], a2.at[1], a2s, a2r, core).wait_recv()
    remote(b2.at[0], b2.at[1], b2s, b2r, core).wait_recv()
    mine[:RA] += a2[1, 0] + a2[1, 1] + a2[1, 2]
    mine[RA:] += b2[1, 0] + b2[1, 1] + b2[1, 2]
    share = RAB // NZ

    def to_z1(k):
        rows = pl.ds(pl.multiple_of(lax.rem(z + k, NZ) * share, 8), share)
        remote(mine.at[rows], z1.at[k - 1], zs, zr, along_z(k)).start()

    ring(to_z1)

    remote(c1, c1, c1s, c1r, core).wait_recv()
    own_rows = pl.ds(pl.multiple_of(RAB + z * 8, 8), 8)
    total = sums[:, own_rows, :]
    for k in range(NZ - 1):
        total += c1[k]
    csum[...] = total

    def block_at(d):
        h, r = lax.div(d, 2), lax.rem(d, 2)
        return 3 - 2 * r - 3 * h + 4 * h * r

    def to_plane(k):
        remote(csum.at[block_at(lax.div(k, NY)) * NY + block_at(lax.rem(k, NY))], c2.at[k - 1], c2s, c2r, on_plane(k)).start()

    plane(to_plane)

    def gather(rows, which):
        def one(k):
            return remote(out_ref.at[rows], out_ref.at[rows], ws.at[which], wr.at[which], along_z(k))

        return one

    rows = pl.ds(pl.multiple_of(z * share, 8), share)
    total = mine[rows, :]
    remote(z1, z1, zs, zr, core).wait()
    for k in range(NZ - 1):
        total += z1[k]
    out_ref[rows, :] = total
    large = gather(rows, 0)
    ring(lambda k: large(k).start())
    total = csum[blocks - 1]
    remote(c2, c2, c2s, c2r, core).wait()
    for k in range(blocks - 1):
        total += c2[k]
    out_ref[own_rows, :] = total
    small = gather(own_rows, 1)
    ring(lambda k: small(k).start())
    remote(z1, z1, ws.at[0], zr, core).wait_send()
    remote(c2.at[pl.ds(0, NZ - 1)], c2.at[pl.ds(0, NZ - 1)], ws.at[1], zr, core).wait_send()
    remote(term.at[1], sums, cs, zr, core).wait_send()
    remote(a1, a1, a1s, zr, core).wait_send()
    remote(b1, b1, b1s, zr, core).wait_send()
    remote(c1, c1, c1s, zr, core).wait_send()
    remote(a2.at[0], a2.at[1], a2s, zr, core).wait_send()
    remote(b2.at[0], b2.at[1], b2s, zr, core).wait_send()
    out_copy.wait()
    remote(z1, z1, zs, wr.at[0], core).wait_recv()
    remote(c2.at[pl.ds(0, NZ - 1)], c2.at[pl.ds(0, NZ - 1)], zs, wr.at[1], core).wait_recv()


def sems(*shape):
    return pltpu.SemaphoreType.DMA(shape) if shape else pltpu.SemaphoreType.DMA


def finish(basis_in, flat, basis_ref, out_ref):
    basis_ref[...] = basis_in[...]
    out_ref[...] = flat[...].T


def local(snapshots, test_matrix):
    basis, flat = pl.pallas_call(
        kernel,
        name="range_finder",
        out_shape=(
            jax.ShapeDtypeStruct((ROWS, RANK), f32),
            jax.ShapeDtypeStruct((RANK, 128), f32),
        ),
        in_specs=[ANY, ANY],
        out_specs=(ANY, VMEM),
        scratch_shapes=[
            pltpu.VMEM((ROWS, SNAPS), bf16),
            pltpu.VMEM((SNAPS, RANK), bf16),
            pltpu.VMEM((ROWS, RANK), f32),
            pltpu.VMEM((2, ROWS, RANK), bf16),
            pltpu.VMEM((ROWS, RANK), f32),
            pltpu.VMEM((2, 128, RANK), f32),
            pltpu.VMEM((128, RANK), f32),
            pltpu.VMEM((15, 8, RANK), f32),
            pltpu.VMEM((NZ, 8, RANK), f32),
            pltpu.VMEM((8, RANK), f32),
            pltpu.VMEM((2, 128, RANK), f32),
            pltpu.VMEM((RANK, 2 * RANK), f32),
            pltpu.VMEM((RANK, RANK), f32),
            pltpu.VMEM((RANK, ROWS), bf16),
            pltpu.VMEM((2, 16, RANK, 128), f32),
            pltpu.VMEM((16, RANK, 128), f32),
            pltpu.VMEM((NY, 3, RA, 128), f32),
            pltpu.VMEM((NX, 3, RB, 128), f32),
            pltpu.VMEM((7, 16, 8, 128), f32),
            pltpu.VMEM((2, 3, RA, 128), f32),
            pltpu.VMEM((2, 3, RB, 128), f32),
            pltpu.VMEM((15, 8, 128), f32),
            pltpu.VMEM((16, 8, 128), f32),
            pltpu.VMEM((RAB, 128), f32),
            pltpu.VMEM((7, RAB // NZ, 128), f32),
            sems(PARTS + 1), sems(),
            sems(), sems(), sems(), sems(), sems(), sems(), sems(), sems(), sems(), sems(),
            sems(), sems(16),
            sems(), sems(NY), sems(), sems(NX), sems(), sems(),
            sems(), sems(), sems(), sems(), sems(), sems(),
            sems(), sems(), sems(2), sems(2),
        ],
        compiler_params=pltpu.CompilerParams(
            collective_id=0, has_side_effects=True, vmem_limit_bytes=56 * 2**20
        ),
    )(snapshots, test_matrix)
    return pl.pallas_call(
        finish,
        name="finish",
        out_shape=(
            jax.ShapeDtypeStruct((ROWS, RANK), f32),
            jax.ShapeDtypeStruct((128, RANK), f32),
        ),
        in_specs=[VMEM, VMEM],
        out_specs=(VMEM, VMEM),
    )(basis, flat)


def solution(mesh):
    return jax.shard_map(
        local,
        mesh=mesh,
        in_specs=(P(("lat", "lon"), None), P()),
        out_specs=(P(("lat", "lon"), None), P("lon", None)),
        check_vma=False,
    )
```

```python
import functools

import jax
import jax.numpy as jnp
from jax import lax
from jax.experimental import pallas as pl
from jax.experimental.pallas import tpu as pltpu
from jax.sharding import PartitionSpec as P

MESH = pl.DeviceIdType.MESH
HIGHEST = lax.Precision.HIGHEST
f32, bf16 = jnp.float32, jnp.bfloat16
VMEM = pl.BlockSpec(memory_space=pltpu.VMEM)
ANY = pl.BlockSpec(memory_space=pl.ANY)

NX, NY, NZ = 4, 4, 8
ROWS, SNAPS, RANK = 1024, 4096, 256
PARTS = 4
PART = ROWS // PARTS
RA, RB, RC = 96, 96, 64
RAB = RA + RB


def place():
    z, lon = lax.axis_index("lat"), lax.axis_index("lon")
    return lax.div(lon, 8), lax.rem(lax.div(lon, 2), 4), z, lax.rem(lon, 2)


def device(x, y, z, c):
    return (z, (x * NY + y) * 2 + c)


def remote(src, dst, send, recv, where):
    return pltpu.make_async_remote_copy(
        src_ref=src, dst_ref=dst, send_sem=send, recv_sem=recv, device_id=where, device_id_type=MESH
    )


def tn(a, b, precision=None):
    return lax.dot_general(a, b, (((0,), (0,)), ((), ())), precision=precision, preferred_element_type=f32)


def nt(a, b, precision=None):
    return lax.dot_general(a, b, (((1,), (1,)), ((), ())), precision=precision, preferred_element_type=f32)


def lanes(v, j):
    return jnp.broadcast_to(v[:, j : j + 1], (8, 128))


def row(v, s):
    return jnp.broadcast_to(v[s : s + 1, :], (8, 128))


def factor_block(d, n=64):
    eye = (
        lax.broadcasted_iota(jnp.int32, (n, n), 0) == lax.broadcasted_iota(jnp.int32, (n, n), 1)
    ).astype(f32)
    both = jnp.concatenate([d, eye], axis=1)
    count = n // 8
    tiles = [both[8 * t : 8 * t + 8] for t in range(count)]
    sub = lax.broadcasted_iota(jnp.int32, (8, 128), 0)
    ahead = [lanes(tiles[0], j) for j in range(8)]
    for p in range(count):
        base = 8 * p
        cols = {p: ahead}
        if p + 1 < count:
            ahead = [lanes(tiles[p + 1], base + 8 + j) for j in range(8)]
        for t in range(p + 1, count):
            cols[t] = [lanes(tiles[t], base + j) for j in range(8)]
        for k in range(8):
            inv = 1.0 / row(cols[p][k], k)
            m = {t: cols[t][k] * inv for t in range(p, count)}
            for j in range(k + 1, 8):
                b = row(cols[p][k], j)
                cols[p][j] = cols[p][j] - (cols[p][k] * b) * inv
                for t in range(p + 1, count):
                    cols[t][j] = cols[t][j] - m[t] * b
            if p + 1 < count:
                for j in range(8):
                    ahead[j] = ahead[j] - m[p + 1] * row(cols[p + 1][k], j)
            pivot_row = row(tiles[p], k)
            if k < 7:
                tiles[p] = tiles[p] - jnp.where(sub > k, m[p], 0.0) * pivot_row
            for t in range(p + 1, count):
                tiles[t] = tiles[t] - m[t] * pivot_row
    both = jnp.concatenate(tiles, axis=0)
    diagonal = jnp.sum(both[:, :n] * eye, axis=1, keepdims=True)
    return both[:, n:] * lax.rsqrt(diagonal)


def kernel(
    snap_ref, test_ref, basis_ref, out_ref,
    snap, test, sketch, split, basis,
    half, from_core, from_xy, from_z, piece, gram, work, inverse,
    flipped, term, sums, a1, b1, c1, a2, b2, c2, csum, mine, z1,
    load, store, gcs, gcr, gxs, gxr, gzs, gzr, gbs, gbr, ghs, ghr,
    cs, cr, a1s, a1r, b1s, b1r, c1s, c1r, a2s, a2r, b2s, b2r, c2s, c2r, zs, zr, ws, wr,
):
    x, y, z, c = place()
    core = device(x, y, z, 1 - c)

    def along_x(d):
        return device(lax.rem(x + d, NX), y, z, c)

    def along_y(d):
        return device(x, lax.rem(y + d, NY), z, c)

    def along_z(d):
        return device(x, y, lax.rem(z + d, NZ), c)

    def on_plane(k):
        return device(lax.rem(x + lax.div(k, NY), NX), lax.rem(y + lax.rem(k, NY), NY), z, c)

    def loop(first, last, body):
        lax.fori_loop(first, last, lambda k, _: (body(k), 0)[1], 0)

    def plane(body):
        loop(0, NX * NY - 1, lambda t: body(1 + lax.rem(25 - t, NX * NY - 1)))

    def ring(body):
        loop(0, NZ - 1, lambda t: body(1 + lax.rem(11 - t, NZ - 1)))

    def part(p):
        rows = pl.ds(pl.multiple_of(p * PART, PART), PART)
        return rows, pltpu.make_async_copy(snap_ref.at[rows], snap.at[rows], load.at[p])

    whole_test = pltpu.make_async_copy(test_ref, test, load.at[PARTS])
    whole_test.start()
    loop(0, PARTS, lambda p: part(p)[1].start())
    barrier = pltpu.get_barrier_semaphore()

    def greet(where):
        pl.semaphore_signal(barrier, inc=1, device_id=where, device_id_type=MESH)

    greet(core)
    plane(lambda k: greet(on_plane(k)))
    ring(lambda k: greet(along_z(k)))
    whole_test.wait()

    def sketch_part(p):
        rows, copy = part(p)
        copy.wait()
        sketch[rows, :] = jnp.dot(snap[rows, :], test[...], preferred_element_type=f32)

    loop(0, PARTS, sketch_part)
    hi = sketch[...].astype(bf16)
    split[0] = hi
    split[1] = (sketch[...] - hi.astype(f32)).astype(bf16)

    def gram_half(h):
        columns = pl.ds(pl.multiple_of(h * 128, 128), 128)
        left = jnp.concatenate([split[0, :, columns], split[1, :, columns]], axis=1)
        r = tn(left, jnp.concatenate([split[0], split[1]], axis=1))
        return (r[:128, :RANK] + r[128:, RANK:]) + (r[:128, RANK:] + r[128:, :RANK])

    halves = remote(half.at[0], from_core, gcs, gcr, core)

    def both_halves(k):
        half[k] = gram_half(lax.rem(c + 1 + k, 2))

        @pl.when(k == 0)
        def _():
            pl.semaphore_wait(barrier, 1 + (NX * NY - 1) + (NZ - 1))
            halves.start()

    loop(0, 2, both_halves)

    work[:, RANK:] = (
        lax.broadcasted_iota(jnp.int32, (RANK, RANK), 0)
        == lax.broadcasted_iota(jnp.int32, (RANK, RANK), 1)
    ).astype(f32)
    halves.wait()
    from_core[...] += half[1]

    def rows_of(cx, cy):
        return pl.ds(pl.multiple_of((cx * NY + cy) * 8, 8), 8)

    def scatter(k):
        rows = rows_of(lax.rem(x + lax.div(k, NY), NX), lax.rem(y + lax.rem(k, NY), NY))
        remote(from_core.at[rows], from_xy.at[k - 1], gxs, gxr, on_plane(k)).start()

    own = rows_of(x, y)
    plane(scatter)
    remote(from_xy, from_xy, gxs, gxr, core).wait()
    total = from_core[own, :]
    for k in range(NX * NY - 1):
        total += from_xy[k]
    piece[...] = total
    ring(lambda k: remote(piece, from_z.at[z], gzs, gzr, along_z(k)).start())
    from_z[z] = total
    remote(from_z.at[pl.ds(0, NZ - 1)], from_z.at[pl.ds(0, NZ - 1)], gzs, gzr, core).wait()
    total = from_z[0]
    for k in range(1, NZ):
        total += from_z[k]
    gram[c, own, :] = total
    mine_of_gram = gram.at[c, own]

    def back(k):
        return remote(mine_of_gram, mine_of_gram, gbs, gbr, on_plane(k))

    plane(lambda k: back(k).start())
    remote(from_xy, from_xy, gbs, gbr, core).wait_recv()
    copy = remote(gram.at[c], gram.at[c], ghs, ghr, core)
    copy.start()
    copy.wait()
    remote(from_xy, from_xy, gbs, gxr, core).wait_send()

    n = 64
    work[:128, :RANK] = gram[0]
    work[128:, :RANK] = gram[1]
    d = work[:n, :n]
    for b in range(RANK // n):
        lo, hi = b * n, (b + 1) * n
        inv = factor_block(d)
        if hi < RANK:
            near = nt(work[hi : hi + n, lo:hi], inv, HIGHEST)
            d = work[hi : hi + n, hi : hi + n] - nt(near, near, HIGHEST)
        r = jnp.dot(inv, work[lo:hi, :], precision=HIGHEST, preferred_element_type=f32)
        inverse[lo:hi, :] = r[:, RANK:]
        if hi < RANK:
            below = nt(work[hi:, lo:hi], inv, HIGHEST)
            work[hi:, :] = work[hi:, :] - jnp.dot(below, r, precision=HIGHEST, preferred_element_type=f32)

    for p in range(PARTS):
        rows = pl.ds(p * PART, PART)
        s = nt(sketch[rows, :], inverse[...], HIGHEST)
        basis[rows, :] = s
        flipped[:, p * PART : (p + 1) * PART] = s.astype(bf16).T
    out_copy = pltpu.make_async_copy(basis, basis_ref, store)
    out_copy.start()

    def off(i):
        h, r = lax.div(i, 2), lax.rem(i, 2)
        return 2 - r + h * (1 + 2 * r)

    to_a, to_b = pl.ds(0, RA), pl.ds(RA, RB)
    blocks = NX * NY
    lag = 4

    def to_core(m):
        return remote(term.at[1, m], sums.at[m], cs, cr.at[m], core)

    def step(n):
        @pl.when(n < blocks)
        def _():
            cx, cy = lax.rem(x + off(lax.div(n, NY)), NX), lax.rem(y + off(lax.rem(n, NY)), NY)
            columns = pl.ds(pl.multiple_of((cx * NY + cy) * 256, 256), 256)
            r = jnp.dot(flipped[...], snap[:, columns], preferred_element_type=f32)
            term[c, n] = r[:, :128]
            term[1 - c, n] = r[:, 128:]
            to_core(n).start()

        @pl.when(n >= lag)
        def _():
            m = n - lag
            i, j = lax.div(m, NY), lax.rem(m, NY)
            to_core(m).wait_recv()
            sums[m] += term[0, m]

            @pl.when(i < NX - 1)
            def _():
                remote(sums.at[m, to_a], a1.at[j, i], a1s, a1r.at[j], along_x(off(i))).start()

            @pl.when(j < NY - 1)
            def _():
                remote(sums.at[m, to_b], b1.at[i, j], b1s, b1r.at[i], along_y(off(j))).start()

            @pl.when(j == NY - 1)
            def _():
                group = pl.ds(pl.multiple_of(i * NY, NY), NY)

                def to_z(k):
                    rows = pl.ds(pl.multiple_of(RAB + lax.rem(z + k, NZ) * 8, 8), 8)
                    remote(sums.at[group, rows], c1.at[k - 1, group], c1s, c1r, along_z(k)).start()

                ring(to_z)

    def steps(g):
        for q in range(4):
            step(g * 4 + q)

    loop(0, (blocks + lag) // 4, steps)

    def a_sum(j):
        remote(a1.at[j], a1.at[j], a1s, a1r.at[j], core).wait_recv()
        return sums[(NX - 1) * NY + j, :RA] + (a1[j, 0] + a1[j, 1] + a1[j, 2])

    def b_sum(i):
        remote(b1.at[i], b1.at[i], b1s, b1r.at[i], core).wait_recv()
        return sums[i * NY + NY - 1, RA:RAB] + (b1[i, 0] + b1[i, 1] + b1[i, 2])

    near = (2, 1, 3)

    def second_a(k):
        a2[0, k] = a_sum(k)
        remote(a2.at[0, k], a2.at[1, k], a2s, a2r, along_y(near[k])).start()

    def second_b(k):
        b2[0, k] = b_sum(k)
        remote(b2.at[0, k], b2.at[1, k], b2s, b2r, along_x(near[k])).start()

    second_b(0)
    second_b(1)
    second_a(0)
    second_a(1)
    second_b(2)
    second_a(2)
    mine[:RA] = a_sum(3)
    mine[RA:] = b_sum(3)
    remote(a2.at[0], a2.at[1], a2s, a2r, core).wait_recv()
    remote(b2.at[0], b2.at[1], b2s, b2r, core).wait_recv()
    mine[:RA] += a2[1, 0] + a2[1, 1] + a2[1, 2]
    mine[RA:] += b2[1, 0] + b2[1, 1] + b2[1, 2]
    share = RAB // NZ

    def to_z1(k):
        rows = pl.ds(pl.multiple_of(lax.rem(z + k, NZ) * share, 8), share)
        remote(mine.at[rows], z1.at[k - 1], zs, zr, along_z(k)).start()

    ring(to_z1)

    remote(c1, c1, c1s, c1r, core).wait_recv()
    own_rows = pl.ds(pl.multiple_of(RAB + z * 8, 8), 8)
    total = sums[:, own_rows, :]
    for k in range(NZ - 1):
        total += c1[k]
    csum[...] = total

    def block_at(d):
        h, r = lax.div(d, 2), lax.rem(d, 2)
        return 3 - 2 * r - 3 * h + 4 * h * r

    def to_plane(k):
        remote(csum.at[block_at(lax.div(k, NY)) * NY + block_at(lax.rem(k, NY))], c2.at[k - 1], c2s, c2r, on_plane(k)).start()

    plane(to_plane)

    def gather(rows, which):
        def one(k):
            return remote(out_ref.at[rows], out_ref.at[rows], ws.at[which], wr.at[which], along_z(k))

        return one

    rows = pl.ds(pl.multiple_of(z * share, 8), share)
    total = mine[rows, :]
    remote(z1, z1, zs, zr, core).wait()
    for k in range(NZ - 1):
        total += z1[k]
    out_ref[rows, :] = total
    large = gather(rows, 0)
    ring(lambda k: large(k).start())
    total = csum[blocks - 1]
    remote(c2, c2, c2s, c2r, core).wait()
    for k in range(blocks - 1):
        total += c2[k]
    out_ref[own_rows, :] = total
    small = gather(own_rows, 1)
    ring(lambda k: small(k).start())
    remote(z1, z1, ws.at[0], zr, core).wait_send()
    remote(c2.at[pl.ds(0, NZ - 1)], c2.at[pl.ds(0, NZ - 1)], ws.at[1], zr, core).wait_send()
    remote(term.at[1], sums, cs, zr, core).wait_send()
    remote(a1, a1, a1s, zr, core).wait_send()
    remote(b1, b1, b1s, zr, core).wait_send()
    remote(c1, c1, c1s, zr, core).wait_send()
    remote(a2.at[0], a2.at[1], a2s, zr, core).wait_send()
    remote(b2.at[0], b2.at[1], b2s, zr, core).wait_send()
    out_copy.wait()
    remote(z1, z1, zs, wr.at[0], core).wait_recv()
    remote(c2.at[pl.ds(0, NZ - 1)], c2.at[pl.ds(0, NZ - 1)], zs, wr.at[1], core).wait_recv()


def sems(*shape):
    return pltpu.SemaphoreType.DMA(shape) if shape else pltpu.SemaphoreType.DMA


def finish(basis_in, flat, basis_ref, out_ref):
    basis_ref[...] = basis_in[...]
    out_ref[...] = flat[...].T


def local(snapshots, test_matrix):
    basis, flat = pl.pallas_call(
        kernel,
        name="range_finder",
        out_shape=(
            jax.ShapeDtypeStruct((ROWS, RANK), f32),
            jax.ShapeDtypeStruct((RANK, 128), f32),
        ),
        in_specs=[ANY, ANY],
        out_specs=(ANY, VMEM),
        scratch_shapes=[
            pltpu.VMEM((ROWS, SNAPS), bf16),
            pltpu.VMEM((SNAPS, RANK), bf16),
            pltpu.VMEM((ROWS, RANK), f32),
            pltpu.VMEM((2, ROWS, RANK), bf16),
            pltpu.VMEM((ROWS, RANK), f32),
            pltpu.VMEM((2, 128, RANK), f32),
            pltpu.VMEM((128, RANK), f32),
            pltpu.VMEM((15, 8, RANK), f32),
            pltpu.VMEM((NZ, 8, RANK), f32),
            pltpu.VMEM((8, RANK), f32),
            pltpu.VMEM((2, 128, RANK), f32),
            pltpu.VMEM((RANK, 2 * RANK), f32),
            pltpu.VMEM((RANK, RANK), f32),
            pltpu.VMEM((RANK, ROWS), bf16),
            pltpu.VMEM((2, 16, RANK, 128), f32),
            pltpu.VMEM((16, RANK, 128), f32),
            pltpu.VMEM((NY, 3, RA, 128), f32),
            pltpu.VMEM((NX, 3, RB, 128), f32),
            pltpu.VMEM((7, 16, 8, 128), f32),
            pltpu.VMEM((2, 3, RA, 128), f32),
            pltpu.VMEM((2, 3, RB, 128), f32),
            pltpu.VMEM((15, 8, 128), f32),
            pltpu.VMEM((16, 8, 128), f32),
            pltpu.VMEM((RAB, 128), f32),
            pltpu.VMEM((7, RAB // NZ, 128), f32),
            sems(PARTS + 1), sems(),
            sems(), sems(), sems(), sems(), sems(), sems(), sems(), sems(), sems(), sems(),
            sems(), sems(16),
            sems(), sems(NY), sems(), sems(NX), sems(), sems(),
            sems(), sems(), sems(), sems(), sems(), sems(),
            sems(), sems(), sems(2), sems(2),
        ],
        compiler_params=pltpu.CompilerParams(
            collective_id=0, has_side_effects=True, vmem_limit_bytes=56 * 2**20
        ),
    )(snapshots, test_matrix)
    return pl.pallas_call(
        finish,
        name="finish",
        out_shape=(
            jax.ShapeDtypeStruct((ROWS, RANK), f32),
            jax.ShapeDtypeStruct((128, RANK), f32),
        ),
        in_specs=[VMEM, VMEM],
        out_specs=(VMEM, VMEM),
    )(basis, flat)


def solution(mesh):
    return jax.shard_map(
        local,
        mesh=mesh,
        in_specs=(P(("lat", "lon"), None), P()),
        out_specs=(P(("lat", "lon"), None), P("lon", None)),
        check_vma=False,
    )
```
